32 devices in a mesh: parts: 2 (over x), tp: 8 (over z, y), ep: 2 (over core).
Axes of the slice: x: 2, y: 2, z: 4, core: 2. Of those that a mesh axis runs over, the one named last changes fastest.
Arguments:
- tokens: bfloat16 [2048, 6144], P(('parts', 'tp')), parts along dimension 0, may hold values from -6 to 6
- expert_ids: int32 [2048, 2], P(('parts', 'tp')), parts along dimension 0, may hold values from 0 to 7, all different within a row; in each aligned block of 128 rows (0 to 127, 128 to 255, ...) at most 36 rows name the same one
- route_weight: float32 [2048, 2], P(('parts', 'tp')), parts along dimension 0, may hold values from 0.2 to 1
- w_gate: bfloat16 [2, 6144, 8192], P('ep', None, 'tp'), may hold values from -0.078125 to 0.078125
- w_up: bfloat16 [2, 6144, 8192], P('ep', None, 'tp'), may hold values from -0.078125 to 0.078125
- w_down: bfloat16 [2, 8192, 6144], P('ep', 'tp'), may hold values from -0.0625 to 0.0625
- round_bits: int32 [2, 8, 288], P('ep', 'tp'), may hold values from 0 to 1073741823
Outputs:
- mixed: bfloat16 [2048, 6144], P(('parts', 'tp'), 'ep'), parts along dimension 0
The draws below stay inside these ranges and needn't reach their ends.
There are 2 independent parts, one for each index of `parts`. The reference program is written for one: setup_inputs(seed, part) draws one part's arguments, and reference() takes and returns one part's arrays. A program takes and returns all parts, laid end to end along the dimension named above; an argument that names none is the same for every part. Nothing has to cross between parts.
Inputs may be any that keep to these rules, and one draw needn't show every extreme that they name: `expert_ids`: A token's 2 ids differ. In each aligned block of 128 tokens (the tokens of one index of tp) no expert is named by more than 36 tokens, and in some blocks some expert is named by exactly 36.
All inputs are finite; a program needn't handle non-finite values.
Results may differ from the reference program's by a relative error of at most 0.015.
Values may be sent and summed in bfloat16 or wider, within the bound.
A program may use at most 128 MiB of HBM per device.

```python
import math
import jax
import jax.numpy as jnp
import numpy as np
from jax import lax

D = 6144
EXPERTS = 8
TOPK = 2
FFW = 8192
TOK_DEV = 128
SLOT = 36
FF_DEV = 1024
TOKENS = 1024
CAPACITY = 288
N_TP = 8
N_EP = 2


def with_ends(drawn, own_key, low, high):
    spot = [jax.random.randint(jax.random.fold_in(own_key, axis), (), 0, length) for axis, length in enumerate(drawn.shape)]
    widest = drawn.shape.index(max(drawn.shape))
    neighbour = spot[:widest] + [(spot[widest] + 1) % drawn.shape[widest]] + spot[widest + 1:]
    return drawn.at[tuple(spot)].set(low).at[tuple(neighbour)].set(high)


def shard_levels(rng, dims, pieces, low, high):
    level = 1.0
    for axis_at, parts in pieces:
        steps = jax.random.uniform(jax.random.fold_in(jax.random.fold_in(rng, 6), axis_at), (parts,), jnp.float32, low / len(pieces), high / len(pieces))
        level = level * jnp.repeat(jnp.exp(steps), dims[axis_at] // parts).reshape((-1,) + (1,) * (len(dims) - 1 - axis_at))
    return level


def shared_out(own_key, own, number, rows, count, top, limit, skew):
    sequence = jax.random.permutation(own_key, count)
    packed, ordinary = portions_of(count, rows * top, limit, skew, True), portions_of(count, rows * top, limit, skew, False)
    places = jnp.arange(count)

    def named(lengths, turn):
        used = int((lengths > 0).sum())
        fixed = max(1, used // 4)
        moved = fixed + (places - fixed + turn * (used - fixed)) % max(1, count - fixed)
        return jnp.zeros((count,), jnp.int32).at[sequence[jnp.where(places < fixed, places, moved)]].set(jnp.asarray(lengths, jnp.int32))

    lengths = jnp.where(number % 4 == 0, named(packed, number // 4), named(ordinary, number - number // 4 - 1))
    mixed = jax.random.permutation(jax.random.fold_in(own, 3), count)
    giver, receiver = mixed[0:count // 2 * 2:2], mixed[1:count // 2 * 2:2]
    margin = jnp.minimum(lengths[giver] - 1, limit - lengths[receiver]) // 2
    margin = jnp.where((giver == sequence[0]) | (receiver == sequence[0]) | (lengths[receiver] == 0), 0, jnp.maximum(margin, 0))
    moved = jax.random.randint(jax.random.fold_in(own, 4), (count // 2,), 0, 1 << 20) % (margin + 1)
    lengths = lengths.at[giver].add(-moved).at[receiver].add(moved)
    labels = jnp.searchsorted(jnp.cumsum(lengths), jnp.arange(rows * top), side="right").astype(jnp.int32)
    listing = labels.reshape(top, rows).T
    listing = listing[jax.random.permutation(jax.random.fold_in(own, 1), rows)]
    turn = jax.random.randint(jax.random.fold_in(own, 2), (rows, 1), 0, top)
    return jnp.take_along_axis(listing, (jnp.arange(top)[None, :] + turn) % top, axis=1)


def portions_of(number_of, total, most, lean, full):
    weights = [(1 << 20) // math.isqrt(rank ** lean) + 1 for rank in range(1, number_of + 1)]
    largest = most if full else min(most, max(-(-total // number_of), total * weights[0] // sum(weights)))
    least = 1 if total - largest >= number_of - 1 else 0
    counts, spare = [largest] + [least] * (number_of - 1), total - largest - least * (number_of - 1)
    while spare > 0:
        movable = [i for i in range(1, number_of) if counts[i] < largest] or [i for i in range(1, number_of) if counts[i] < most]
        pool, remaining = sum([weights[i] for i in movable]), spare
        for i in movable:
            extra = min(most - counts[i], max(1, remaining * weights[i] // pool), spare)
            counts[i] = counts[i] + extra
            spare = spare - extra
    return np.array(counts)


def gaussian(rng, extent, width, reach, split=(), held_as=jnp.bfloat16):
    gain = shard_levels(rng, extent, split, -0.22, 0.18) if split else 1.0
    entries = jax.random.normal(rng, extent, jnp.float32) * width * gain
    return jnp.minimum(jnp.maximum(entries, -reach), reach).astype(held_as)


def setup_inputs(seed: int = 0, part: int = 0) -> dict:
    streams_of = jax.random.split(jax.random.key(seed), 8)
    part_splits = jax.random.split(jax.random.fold_in(streams_of[7], part), 8)
    tokens = gaussian(part_splits[0], (TOKENS, D), 1.0, 6.0, ((0, 8),))
    expert_ids_keys = jax.random.split(jax.random.fold_in(part_splits[1], 1), TOKENS // TOK_DEV)
    expert_ids_turns = jax.random.permutation(jax.random.fold_in(part_splits[1], 3), TOKENS // TOK_DEV)
    expert_ids = jax.vmap(lambda own, number: shared_out(jax.random.fold_in(part_splits[1], 2), own, number, TOK_DEV, EXPERTS, TOPK, SLOT, 2))(expert_ids_keys, expert_ids_turns).reshape((TOKENS, TOPK))
    route_weight = jnp.clip(0.2 + 0.8 * jax.random.uniform(part_splits[2], (TOKENS, TOPK), jnp.float32) ** shard_levels(part_splits[2], (TOKENS, TOPK), ((0, 8),), -0.2, 0.2), 0.2, 1.0)
    w_gate = gaussian(streams_of[3], (N_EP, D, FFW), D ** -0.5, 0.078125, ((0, 2), (2, 8)))
    w_up = gaussian(streams_of[4], (N_EP, D, FFW), D ** -0.5, 0.078125, ((0, 2), (2, 8)))
    w_down = gaussian(streams_of[5], (N_EP, FFW, D), FFW ** -0.5, 0.0625, ((0, 2), (1, 8)))
    round_bits = with_ends(jax.random.randint(streams_of[6], (N_EP, N_TP, CAPACITY), 0, 1073741824), jax.random.fold_in(streams_of[6], 1), 0, 1073741823).astype(jnp.int32)
    return {"tokens": tokens, "expert_ids": expert_ids, "route_weight": route_weight, "w_gate": w_gate, "w_up": w_up, "w_down": w_down, "round_bits": round_bits}


def dither(partial_value, row_bits):
    columns = jnp.arange(partial_value.shape[1], dtype=jnp.int32)
    mixed_bits = (row_bits[:, None] + 40503 * columns[None, :]) % 65536
    factor = 0.5 + mixed_bits.astype(jnp.float32) / 65536.0
    return (partial_value * factor).astype(jnp.bfloat16)


def reference(tokens, expert_ids, route_weight, w_gate, w_up, w_down, round_bits):
    capacity = N_TP * SLOT
    grouped = expert_ids.reshape(N_TP, TOK_DEV, TOPK)
    weights_grouped = route_weight.reshape(N_TP, TOK_DEV, TOPK)
    output = jnp.zeros((TOKENS, D), jnp.float32)
    for e in range(N_EP):
        chosen = grouped == e
        targeted = jnp.any(chosen, axis=2)
        ordinal = jnp.cumsum(targeted.astype(jnp.int32), axis=1) - 1
        row_index = jnp.arange(N_TP, dtype=jnp.int32)[:, None] * SLOT + ordinal
        row_index = jnp.where(targeted, row_index, capacity).reshape(-1).astype(jnp.int32)
        expert_rows = jnp.zeros((capacity, D), jnp.bfloat16).at[row_index].set(tokens, mode="drop")
        gate_act = jnp.dot(expert_rows, w_gate[e], preferred_element_type=jnp.float32)
        up_act = jnp.dot(expert_rows, w_up[e], preferred_element_type=jnp.float32)
        hidden = (jax.nn.silu(gate_act) * up_act).astype(jnp.bfloat16)
        hidden_parts = hidden.reshape(capacity, N_TP, FF_DEV).transpose(1, 0, 2)
        down_parts = w_down[e].reshape(N_TP, FF_DEV, D)

        def accumulate(total, inputs):
            hidden_slice, down_slice, row_bits = inputs
            partial_value = jnp.dot(hidden_slice, down_slice, preferred_element_type=jnp.float32)
            return total + dither(partial_value, row_bits).astype(jnp.float32), None

        total, _ = lax.scan(accumulate, jnp.zeros((capacity, D), jnp.float32),
                            (hidden_parts, down_parts, round_bits[e]))
        expert_out = total.astype(jnp.bfloat16)
        weight_e = jnp.sum(jnp.where(chosen, weights_grouped, 0.0), axis=2).reshape(-1)
        picked = expert_out[jnp.minimum(row_index, capacity - 1)].astype(jnp.float32)
        output = output + weight_e[:, None] * picked
    return output.astype(jnp.bfloat16)
```

```python
import functools

import jax
import jax.numpy as jnp
from jax import lax
from jax.experimental import pallas as pl
from jax.experimental.pallas import tpu as pltpu
from jax.sharding import PartitionSpec as P

SLOT = 36
MAIN = 32
REST = SLOT - MAIN
PACK = MAIN // REST
PAIR = 2 * MAIN + 16
F32 = jnp.float32
BF16 = jnp.bfloat16


def mm(a, b, dims=((1,), (0,))):
    return lax.dot_general(a, b, (dims, ((), ())), preferred_element_type=F32)


def one_hot(rows, cols, test):
    r = lax.broadcasted_iota(jnp.int32, (rows, cols), 0)
    c = lax.broadcasted_iota(jnp.int32, (rows, cols), 1)
    return jnp.where(test(r, c), 1.0, 0.0).astype(BF16)


def kernel(
    n, tok, ids, wts, bits, wg_hbm, wu_hbm, wd_hbm, out,
    wg, wu, wd, X, xl, h, pb, yr, zr, em, ex,
    wsem, sR, sL, sY, rz, ry, sYr, rYr, sZ, rL, rR, se, re,
):
    nz = n // 2
    t = lax.axis_index("tp")
    e = lax.axis_index("ep")
    z, y = t // 2, t % 2
    D = tok.shape[1]
    CH = D // PACK
    F = wg.shape[1]
    TOK = tok.shape[0]
    partner = t + 1 - 2 * y
    first, last = z == 0, z == nz - 1

    loads = [
        pltpu.make_async_copy(a.at[0], b, wsem.at[i])
        for i, (a, b) in enumerate(((wg_hbm, wg), (wu_hbm, wu), (wd_hbm, wd)))
    ]
    for c in loads:
        c.start()

    barrier = pltpu.get_barrier_semaphore()
    pl.semaphore_signal(barrier, inc=1, device_id={"tp": partner})
    pl.semaphore_signal(barrier, inc=1, device_id={"ep": 1 - e})

    @pl.when(jnp.logical_not(first))
    def _():
        pl.semaphore_signal(barrier, inc=1, device_id={"tp": t - 2})

    @pl.when(jnp.logical_not(last))
    def _():
        pl.semaphore_signal(barrier, inc=1, device_id={"tp": t + 2})

    tri = one_hot(TOK, TOK, lambda r, c: c <= r)

    def routing(expert):
        hit = ids[...] == expert
        share = jnp.sum(jnp.where(hit, wts[...], 0.0), axis=1, keepdims=True)
        named = jnp.sum(jnp.where(hit, 1.0, 0.0), axis=1, keepdims=True)
        named = jnp.broadcast_to(named, (TOK, TOK))
        count = mm(tri, named.astype(BF16))
        row = jnp.where(named > 0.5, count, 0.0).astype(jnp.int32) - 1
        return share, row

    def main_hot(row):
        c = lax.broadcasted_iota(jnp.int32, (TOK, MAIN), 1)
        return jnp.where(row[:, :MAIN] == c, 1.0, 0.0).astype(BF16)

    def rest_hot(row, q, width):
        c = lax.broadcasted_iota(jnp.int32, (TOK, width), 1)
        here = (c >= REST * q) & (c < REST * q + REST)
        return jnp.where(here & (row[:, :width] - MAIN == c - REST * q), 1.0, 0.0).astype(BF16)

    _, row = routing(e)
    hot = main_hot(row)
    rest = jnp.zeros((MAIN, CH), F32)
    for q in range(PACK):
        part = tok[:, q * CH:(q + 1) * CH]
        X[t, :, q * CH:(q + 1) * CH] = mm(hot, part, ((0,), (0,))).astype(BF16)
        rest = rest + mm(rest_hot(row, q, MAIN), part, ((0,), (0,)))
    X[t, :, D:] = rest.astype(BF16)

    neighbours = 4 - first.astype(jnp.int32) - last.astype(jnp.int32)
    pl.semaphore_wait(barrier, neighbours)

    def go_right(b):
        i = 2 * b + y
        return pltpu.make_async_remote_copy(X.at[i], X.at[i], sR.at[b], rz.at[b], device_id={"tp": t + 2})

    def go_left(b):
        i = 2 * b + y
        return pltpu.make_async_remote_copy(X.at[i], X.at[i], sL.at[b], rz.at[b], device_id={"tp": t - 2})

    def go_y(b):
        i = 2 * b + y
        return pltpu.make_async_remote_copy(X.at[i], X.at[i], sY.at[b], ry.at[b], device_id={"tp": partner})

    @pl.when(jnp.logical_not(last))
    def _():
        go_right(z).start()

    @pl.when(jnp.logical_not(first))
    def _():
        go_left(z).start()

    go_y(z).start()

    def arrivals(d):
        a, b = z - d, z + d

        @pl.when(a >= 0)
        def _():
            go_right(a).wait_recv()

            @pl.when(jnp.logical_not(last))
            def _():
                go_right(a).start()

            go_y(a).start()

        @pl.when(b < nz)
        def _():
            go_left(b).wait_recv()

            @pl.when(jnp.logical_not(first))
            def _():
                go_left(b).start()

            go_y(b).start()

    def place(j):
        d = (j + 1) // 2
        return jnp.where(j % 2 == 1, z - d, z + d)

    def hidden(b):
        go_y(b).wait_recv()
        packed = X[pl.ds(2 * b, 2), :, D:].reshape(2 * MAIN, CH)
        for q in range(PACK):
            pick = one_hot(16, 2 * MAIN, lambda r, c: (r < 2 * REST) & (c == (r // REST) * MAIN + REST * q + r % REST))
            cols = slice(q * CH, (q + 1) * CH)
            xl[:2 * MAIN, cols] = X[pl.ds(2 * b, 2), :, cols].reshape(2 * MAIN, CH)
            xl[2 * MAIN:, cols] = mm(pick, packed).astype(BF16)

        def tile(i, _):
            cols = pl.ds(pl.multiple_of(i * 256, 256), 256)
            g = mm(xl[...], wg[:, cols])
            u = mm(xl[...], wu[:, cols])
            h[b, :, cols] = ((g / (1.0 + jnp.exp(-g))) * u).astype(BF16)
            return 0

        lax.fori_loop(0, F // 256, tile, 0)

    arrivals(1)
    loads[0].wait()
    loads[1].wait()

    def gather_step(j, _):
        d = (j + 1) // 2 + 1

        @pl.when((j % 2 == 1) & (d < nz))
        def _():
            arrivals(d)

        b = place(j)

        @pl.when((b >= 0) & (b < nz))
        def _():
            hidden(b)

        return 0

    lax.fori_loop(0, 2 * nz - 1, gather_step, 0)
    loads[2].wait()

    def give_y(b):
        return pltpu.make_async_remote_copy(
            pb.at[2 * b + 1 - y], yr.at[b], sYr.at[b], rYr.at[b], device_id={"tp": partner})

    def give_right(b):
        return pltpu.make_async_remote_copy(
            pb.at[2 * b + y], zr.at[b + 1], sZ.at[b], rL.at[b], device_id={"tp": t + 2})

    def give_left(b):
        return pltpu.make_async_remote_copy(
            pb.at[2 * b + y], zr.at[b], sZ.at[b], rR.at[b], device_id={"tp": t - 2})

    def down(b):
        rest = jnp.zeros((2 * MAIN, CH), F32)
        for q in range(PACK):
            cols = slice(q * CH, (q + 1) * CH)
            part = mm(h[b], wd[:, cols])
            c = lax.broadcasted_iota(jnp.int32, (PAIR, CH), 1) + q * CH
            low = (bits[b] + 40503 * c) & 65535
            part = (part * (0.5 + low.astype(F32) / 65536.0)).astype(BF16)
            pb[pl.ds(2 * b, 2), :, cols] = part[:2 * MAIN].reshape(2, MAIN, CH)
            put = one_hot(2 * MAIN, 16, lambda r, c: (c < 2 * REST) & (r == (c // REST) * MAIN + REST * q + c % REST))
            rest = rest + mm(put, part[2 * MAIN:])
        pb[pl.ds(2 * b, 2), :, D:] = rest.astype(BF16).reshape(2, MAIN, CH)
        give_y(b).start()

    def down_step(i, _):
        b = place(2 * nz - 2 - i)

        @pl.when((b >= 0) & (b < nz))
        def _():
            down(b)

        return 0

    lax.fori_loop(0, 2 * nz - 1, down_step, 0)

    def add_all(i, more):
        for q in range(PACK + 1):
            cols = slice(q * CH, (q + 1) * CH)
            total = pb[i, :, cols].astype(F32)
            for ref, k in more:
                total = total + ref[k, :, cols].astype(F32)
            pb[i, :, cols] = total.astype(BF16)

    def reduce_step(i, _):
        b = place(2 * nz - 2 - i)
        mine = 2 * b + y

        @pl.when((b >= 0) & (b < nz))
        def _():
            give_y(b).wait_recv()

            @pl.when((b >= z) & jnp.logical_not(first))
            def _():
                give_right(b).wait_recv()

            @pl.when((b <= z) & jnp.logical_not(last))
            def _():
                give_left(b).wait_recv()

            @pl.when(((b > z) & first) | ((b < z) & last))
            def _():
                add_all(mine, ((yr, b),))

            @pl.when(((b > z) & jnp.logical_not(first)) | ((b == z) & last))
            def _():
                add_all(mine, ((yr, b), (zr, b + 1)))

            @pl.when(((b < z) & jnp.logical_not(last)) | ((b == z) & first))
            def _():
                add_all(mine, ((yr, b), (zr, b)))

            @pl.when((b == z) & jnp.logical_not(first) & jnp.logical_not(last))
            def _():
                add_all(mine, ((yr, b), (zr, b + 1), (zr, b)))

            @pl.when(b > z)
            def _():
                give_right(b).start()

            @pl.when(b < z)
            def _():
                give_left(b).start()

        return 0

    lax.fori_loop(0, 2 * nz - 1, reduce_step, 0)

    half = D // 2
    theirs = pl.ds(pl.multiple_of((1 - e) * half, 128), half)
    give_main = pltpu.make_async_remote_copy(
        pb.at[t, :, theirs], em, se.at[0], re.at[0], device_id={"ep": 1 - e})
    give_rest = pltpu.make_async_remote_copy(
        pb.at[t, pl.ds(pl.multiple_of((1 - e) * 16, 16), 16), D:], ex, se.at[1], re.at[1], device_id={"ep": 1 - e})
    give_main.start()
    give_rest.start()
    share0, row0 = routing(e)
    share1, row1 = routing(1 - e)
    hot0, hot1 = main_hot(row0), main_hot(row1)
    give_main.wait_recv()
    give_rest.wait_recv()
    rest0 = pb[t, pl.ds(pl.multiple_of(e * 16, 16), 16), D:]
    rest1 = ex[...]
    for q in range(PACK // 2):
        cols = slice(q * CH, (q + 1) * CH)
        own = pl.ds(pl.multiple_of(e * half + q * CH, 128), CH)
        a = mm(hot0, pb[t, :, own]) + mm(rest_hot(row0, q, 16), rest0)
        b = mm(hot1, em[:, cols]) + mm(rest_hot(row1, q, 16), rest1)
        out[:, cols] = (share0 * a + share1 * b).astype(BF16)

    give_main.wait_send()
    give_rest.wait_send()

    def finish(b, _):
        go_y(b).wait_send()
        give_y(b).wait_send()

        @pl.when((b <= z) & jnp.logical_not(last))
        def _():
            go_right(b).wait_send()

        @pl.when((b >= z) & jnp.logical_not(first))
        def _():
            go_left(b).wait_send()

        @pl.when(b > z)
        def _():
            give_right(b).wait_send()

        @pl.when(b < z)
        def _():
            give_left(b).wait_send()

        return 0

    lax.fori_loop(0, nz, finish, 0)


def shards(n, tokens, expert_ids, route_weight, w_gate, w_up, w_down, round_bits):
    nz = n // 2
    D = tokens.shape[1]
    F = w_gate.shape[2]
    wide = D + D // PACK
    rows = round_bits.reshape(nz, 2, SLOT)
    main = rows[:, :, :MAIN].reshape(nz, 2 * MAIN)
    rest = rows[:, :, MAIN:].reshape(nz, 2 * REST)
    bits = jnp.concatenate([main, rest, jnp.zeros((nz, 16 - 2 * REST), jnp.int32)], axis=1)[:, :, None]
    vmem = pl.BlockSpec(memory_space=pltpu.VMEM)
    hbm = pl.BlockSpec(memory_space=pl.ANY)
    dma = pltpu.SemaphoreType.DMA
    return pl.pallas_call(
        functools.partial(kernel, n),
        out_shape=jax.ShapeDtypeStruct((tokens.shape[0], D // 2), BF16),
        in_specs=[vmem] * 4 + [hbm] * 3,
        out_specs=vmem,
        scratch_shapes=[
            pltpu.VMEM((D, F), BF16),
            pltpu.VMEM((D, F), BF16),
            pltpu.VMEM((F, D), BF16),
            pltpu.VMEM((n, MAIN, wide), BF16),
            pltpu.VMEM((PAIR, D), BF16),
            pltpu.VMEM((nz, PAIR, F), BF16),
            pltpu.VMEM((n, MAIN, wide), BF16),
            pltpu.VMEM((nz, MAIN, wide), BF16),
            pltpu.VMEM((nz + 1, MAIN, wide), BF16),
            pltpu.VMEM((MAIN, D // 2), BF16),
            pltpu.VMEM((16, D // PACK), BF16),
            dma((3,)),
        ] + [dma((nz,))] * 10 + [dma((2,))] * 2,
        compiler_params=pltpu.CompilerParams(
            collective_id=0, has_side_effects=True, vmem_limit_bytes=62 * 2**20
        ),
        cost_estimate=pl.CostEstimate(
            flops=6 * n * SLOT * D * F, bytes_accessed=6 * D * F, transcendentals=n * SLOT * F
        ),
    )(tokens, expert_ids, route_weight, bits, w_gate, w_up, w_down)


def solution(mesh):
    return jax.shard_map(
        functools.partial(shards, mesh.shape["tp"]),
        mesh=mesh,
        in_specs=(
            P(("parts", "tp"), None),
            P(("parts", "tp"), None),
            P(("parts", "tp"), None),
            P("ep", None, "tp"),
            P("ep", None, "tp"),
            P("ep", "tp", None),
            P("ep", "tp", None),
        ),
        out_specs=P(("parts", "tp"), "ep"),
        check_vma=False,
    )
```

```python
import functools

import jax
import jax.numpy as jnp
from jax import lax
from jax.experimental import pallas as pl
from jax.experimental.pallas import tpu as pltpu
from jax.sharding import PartitionSpec as P

SLOT = 36
MAIN = 32
REST = SLOT - MAIN
PACK = MAIN // REST
PAIR = 2 * MAIN + 16
F32 = jnp.float32
BF16 = jnp.bfloat16


def mm(a, b, dims=((1,), (0,))):
    return lax.dot_general(a, b, (dims, ((), ())), preferred_element_type=F32)


def one_hot(rows, cols, test):
    r = lax.broadcasted_iota(jnp.int32, (rows, cols), 0)
    c = lax.broadcasted_iota(jnp.int32, (rows, cols), 1)
    return jnp.where(test(r, c), 1.0, 0.0).astype(BF16)


def kernel(
    n, cut, tok, ids, wts, bits, wg_hbm, wu_hbm, wd_hbm, out,
    wg, wu, wd, X, xl, h, pb, yr, zr, zt, yt, em, ex,
    wsem, sR, sL, sY, rz, ry, sYr, rYr, sZ, rL, rR, sRt, sLt, rzt, sZt, rLt, rRt, st, rt, se, re,
):
    nz = n // 2
    t = lax.axis_index("tp")
    e = lax.axis_index("ep")
    z, y = t // 2, t % 2
    D = tok.shape[1]
    CH = D // PACK
    F = wg.shape[1]
    TOK = tok.shape[0]
    partner = t + 1 - 2 * y
    first, last = z == 0, z == nz - 1

    loads = [
        pltpu.make_async_copy(a.at[0], b, wsem.at[i])
        for i, (a, b) in enumerate(((wg_hbm, wg), (wu_hbm, wu), (wd_hbm, wd)))
    ]
    for c in loads:
        c.start()

    barrier = pltpu.get_barrier_semaphore()
    pl.semaphore_signal(barrier, inc=1, device_id={"tp": partner})
    pl.semaphore_signal(barrier, inc=1, device_id={"ep": 1 - e})

    @pl.when(jnp.logical_not(first))
    def _():
        pl.semaphore_signal(barrier, inc=1, device_id={"tp": t - 2})

    @pl.when(jnp.logical_not(last))
    def _():
        pl.semaphore_signal(barrier, inc=1, device_id={"tp": t + 2})

    tri = one_hot(TOK, TOK, lambda r, c: c <= r)

    def routing(expert):
        hit = ids[...] == expert
        share = jnp.sum(jnp.where(hit, wts[...], 0.0), axis=0, keepdims=True)
        named = jnp.sum(jnp.where(hit, 1.0, 0.0), axis=0, keepdims=True)
        share = jnp.broadcast_to(share, (TOK, TOK)).T[:, :1]
        named = jnp.broadcast_to(named, (TOK, TOK)).T
        count = mm(tri, named.astype(BF16))
        row = jnp.where(named > 0.5, count, 0.0).astype(jnp.int32) - 1
        return share, row

    def main_hot(row):
        c = lax.broadcasted_iota(jnp.int32, (TOK, MAIN), 1)
        return jnp.where(row[:, :MAIN] == c, 1.0, 0.0).astype(BF16)

    def rest_hot(row, q, width):
        c = lax.broadcasted_iota(jnp.int32, (TOK, width), 1)
        here = (c >= REST * q) & (c < REST * q + REST)
        return jnp.where(here & (row[:, :width] - MAIN == c - REST * q), 1.0, 0.0).astype(BF16)

    _, row = routing(e)
    hot = main_hot(row)
    rest = jnp.zeros((MAIN, CH), F32)
    for q in range(PACK):
        part = tok[:, q * CH:(q + 1) * CH]
        X[t, :, q * CH:(q + 1) * CH] = mm(hot, part, ((0,), (0,))).astype(BF16)
        rest = rest + mm(rest_hot(row, q, MAIN), part, ((0,), (0,)))
    X[t, :, D:] = rest.astype(BF16)

    neighbours = 4 - first.astype(jnp.int32) - last.astype(jnp.int32)
    pl.semaphore_wait(barrier, neighbours)

    def go_right(b):
        i = 2 * b + y
        return pltpu.make_async_remote_copy(X.at[i], X.at[i], sR.at[b], rz.at[b], device_id={"tp": t + 2})

    def go_left(b):
        i = 2 * b + y
        return pltpu.make_async_remote_copy(X.at[i], X.at[i], sL.at[b], rz.at[b], device_id={"tp": t - 2})

    def go_y(b):
        i = 2 * b + y
        return pltpu.make_async_remote_copy(
            X.at[i, :, :cut], X.at[i, :, :cut], sY.at[b], ry.at[b], device_id={"tp": partner})

    def tail_y():
        return pltpu.make_async_remote_copy(
            X.at[t, :, cut:], X.at[t, :, cut:], st.at[0], rt.at[0], device_id={"tp": partner})

    def tail_right(b):
        i = 2 * b + 1 - y
        return pltpu.make_async_remote_copy(
            X.at[i, :, cut:], X.at[i, :, cut:], sRt.at[b], rzt.at[b], device_id={"tp": t + 2})

    def tail_left(b):
        i = 2 * b + 1 - y
        return pltpu.make_async_remote_copy(
            X.at[i, :, cut:], X.at[i, :, cut:], sLt.at[b], rzt.at[b], device_id={"tp": t - 2})

    tail_y().start()
    go_y(z).start()

    @pl.when(jnp.logical_not(last))
    def _():
        go_right(z).start()

    @pl.when(jnp.logical_not(first))
    def _():
        go_left(z).start()

    tail_y().wait_recv()

    @pl.when(jnp.logical_not(last))
    def _():
        tail_right(z).start()

    @pl.when(jnp.logical_not(first))
    def _():
        tail_left(z).start()

    def arrivals(d):
        a, b = z - d, z + d

        @pl.when(a >= 0)
        def _():
            go_right(a).wait_recv()

            @pl.when(jnp.logical_not(last))
            def _():
                go_right(a).start()

            go_y(a).start()
            tail_right(a).wait_recv()

            @pl.when(jnp.logical_not(last))
            def _():
                tail_right(a).start()

        @pl.when(b < nz)
        def _():
            go_left(b).wait_recv()

            @pl.when(jnp.logical_not(first))
            def _():
                go_left(b).start()

            go_y(b).start()
            tail_left(b).wait_recv()

            @pl.when(jnp.logical_not(first))
            def _():
                tail_left(b).start()

    def place(j):
        d = (j + 1) // 2
        return jnp.where(j % 2 == 1, z - d, z + d)

    def hidden(b):
        go_y(b).wait_recv()
        packed = X[pl.ds(2 * b, 2), :, D:].reshape(2 * MAIN, CH)
        for q in range(PACK):
            pick = one_hot(16, 2 * MAIN, lambda r, c: (r < 2 * REST) & (c == (r // REST) * MAIN + REST * q + r % REST))
            cols = slice(q * CH, (q + 1) * CH)
            xl[:2 * MAIN, cols] = X[pl.ds(2 * b, 2), :, cols].reshape(2 * MAIN, CH)
            xl[2 * MAIN:, cols] = mm(pick, packed).astype(BF16)

        def tile(i, _):
            cols = pl.ds(pl.multiple_of(i * 256, 256), 256)
            g = mm(xl[...], wg[:, cols])
            u = mm(xl[...], wu[:, cols])
            h[b, :, cols] = ((g / (1.0 + jnp.exp(-g))) * u).astype(BF16)
            return 0

        lax.fori_loop(0, F // 256, tile, 0)

    arrivals(1)
    loads[0].wait()
    loads[1].wait()

    def gather_step(j, _):
        d = (j + 1) // 2 + 1

        @pl.when((j % 2 == 1) & (d < nz))
        def _():
            arrivals(d)

        b = place(j)

        @pl.when((b >= 0) & (b < nz))
        def _():
            hidden(b)

        return 0

    lax.fori_loop(0, 2 * nz - 1, gather_step, 0)
    loads[2].wait()

    def give_y(b):
        return pltpu.make_async_remote_copy(
            pb.at[2 * b + 1 - y, :, :cut], yr.at[b], sYr.at[b], rYr.at[b], device_id={"tp": partner})

    def give_right(b):
        return pltpu.make_async_remote_copy(
            pb.at[2 * b + y], zr.at[b + 1], sZ.at[b], rL.at[b], device_id={"tp": t + 2})

    def give_left(b):
        return pltpu.make_async_remote_copy(
            pb.at[2 * b + y], zr.at[b], sZ.at[b], rR.at[b], device_id={"tp": t - 2})

    def tail_give_right(b):
        return pltpu.make_async_remote_copy(
            pb.at[2 * b + 1 - y, :, cut:], zt.at[b + 1], sZt.at[b], rLt.at[b], device_id={"tp": t + 2})

    def tail_give_left(b):
        return pltpu.make_async_remote_copy(
            pb.at[2 * b + 1 - y, :, cut:], zt.at[b], sZt.at[b], rRt.at[b], device_id={"tp": t - 2})

    def tail_give_y():
        return pltpu.make_async_remote_copy(
            pb.at[partner, :, cut:], yt, st.at[1], rt.at[1], device_id={"tp": partner})

    low16 = (bits[0] & 65535).astype(F32)

    def row_noise(b):
        shape = (PAIR, n * SLOT)
        r = lax.broadcasted_iota(jnp.int32, shape, 0)
        c = lax.broadcasted_iota(jnp.int32, shape, 1) - 2 * SLOT * b
        k = r - 2 * MAIN
        main = (r // MAIN) * SLOT + r % MAIN
        rest = (k // REST) * SLOT + MAIN + k % REST
        source = jnp.where(r < 2 * MAIN, main, jnp.where(k < 2 * REST, rest, -n * SLOT - 1))
        picked = jnp.where(source == c, jnp.broadcast_to(low16, shape), 0.0)
        return jnp.sum(picked, axis=1, keepdims=True).astype(jnp.int32)

    def down(b):
        noise = row_noise(b)
        rest = jnp.zeros((2 * MAIN, CH), F32)
        for q in range(PACK):
            cols = slice(q * CH, (q + 1) * CH)
            part = mm(h[b], wd[:, cols])
            c = lax.broadcasted_iota(jnp.int32, (PAIR, CH), 1) + q * CH
            low = (noise + 40503 * c) & 65535
            part = (part * (0.5 + low.astype(F32) / 65536.0)).astype(BF16)
            pb[pl.ds(2 * b, 2), :, cols] = part[:2 * MAIN].reshape(2, MAIN, CH)
            put = one_hot(2 * MAIN, 16, lambda r, c: (c < 2 * REST) & (r == (c // REST) * MAIN + REST * q + c % REST))
            rest = rest + mm(put, part[2 * MAIN:])
        pb[pl.ds(2 * b, 2), :, D:] = rest.astype(BF16).reshape(2, MAIN, CH)
        give_y(b).start()

    def add_in(i, start, stop, terms):
        for c in range(start, stop, 384):
            size = min(384, stop - c)
            total = pb[i, :, c:c + size].astype(F32)
            for ref, k, base in terms:
                total = total + ref[k, :, c - base:c - base + size].astype(F32)
            pb[i, :, c:c + size] = total.astype(BF16)

    wide = pb.shape[2]

    def reduce(b):
        mine, other = 2 * b + y, 2 * b + 1 - y
        from_left = (b >= z) & jnp.logical_not(first)
        from_right = (b <= z) & jnp.logical_not(last)
        only_left = from_left & jnp.logical_not(from_right)
        only_right = from_right & jnp.logical_not(from_left)
        both = from_left & from_right
        none = jnp.logical_not(from_left) & jnp.logical_not(from_right)

        @pl.when(from_left)
        def _():
            tail_give_right(b).wait_recv()

        @pl.when(from_right)
        def _():
            tail_give_left(b).wait_recv()

        @pl.when(only_left)
        def _():
            add_in(other, cut, wide, ((zt, b + 1, cut),))

        @pl.when(only_right)
        def _():
            add_in(other, cut, wide, ((zt, b, cut),))

        @pl.when(both)
        def _():
            add_in(other, cut, wide, ((zt, b + 1, cut), (zt, b, cut)))

        @pl.when(b > z)
        def _():
            tail_give_right(b).start()

        @pl.when(b < z)
        def _():
            tail_give_left(b).start()

        @pl.when(b == z)
        def _():
            tail_give_y().start()

        give_y(b).wait_recv()

        @pl.when(from_left)
        def _():
            give_right(b).wait_recv()

        @pl.when(from_right)
        def _():
            give_left(b).wait_recv()

        @pl.when(none)
        def _():
            add_in(mine, 0, cut, ((yr, b, 0),))

        @pl.when(only_left)
        def _():
            add_in(mine, 0, cut, ((yr, b, 0), (zr, b + 1, 0)))
            add_in(mine, cut, wide, ((zr, b + 1, 0),))

        @pl.when(only_right)
        def _():
            add_in(mine, 0, cut, ((yr, b, 0), (zr, b, 0)))
            add_in(mine, cut, wide, ((zr, b, 0),))

        @pl.when(both)
        def _():
            add_in(mine, 0, cut, ((yr, b, 0), (zr, b + 1, 0), (zr, b, 0)))
            add_in(mine, cut, wide, ((zr, b + 1, 0), (zr, b, 0)))

        @pl.when(b > z)
        def _():
            give_right(b).start()

        @pl.when(b < z)
        def _():
            give_left(b).start()

    steps, lag = 2 * nz - 1, 3

    def down_step(i, _):
        b = place(jnp.maximum(steps - 1 - i, 0))

        @pl.when((i < steps) & (b >= 0) & (b < nz))
        def _():
            down(b)

        k = place(jnp.minimum(steps - 1 - i + lag, steps - 1))

        @pl.when((i >= lag) & (k >= 0) & (k < nz))
        def _():
            reduce(k)

        return 0

    lax.fori_loop(0, steps + lag, down_step, 0)
    tail_give_y().wait_recv()
    for c in range(cut, wide, 384):
        size = min(384, wide - c)
        pb[t, :, c:c + size] = (
            pb[t, :, c:c + size].astype(F32) + yt[:, c - cut:c - cut + size].astype(F32)
        ).astype(BF16)

    half = D // 2
    theirs = pl.ds(pl.multiple_of((1 - e) * half, 128), half)
    give_main = pltpu.make_async_remote_copy(
        pb.at[t, :, theirs], em, se.at[0], re.at[0], device_id={"ep": 1 - e})
    give_rest = pltpu.make_async_remote_copy(
        pb.at[t, pl.ds(pl.multiple_of((1 - e) * 16, 16), 16), D:], ex, se.at[1], re.at[1], device_id={"ep": 1 - e})
    give_main.start()
    give_rest.start()
    share0, row0 = routing(e)
    share1, row1 = routing(1 - e)
    hot0, hot1 = main_hot(row0), main_hot(row1)
    give_main.wait_recv()
    give_rest.wait_recv()
    rest0 = pb[t, pl.ds(pl.multiple_of(e * 16, 16), 16), D:]
    rest1 = ex[...]
    for q in range(PACK // 2):
        cols = slice(q * CH, (q + 1) * CH)
        own = pl.ds(pl.multiple_of(e * half + q * CH, 128), CH)
        a = mm(hot0, pb[t, :, own]) + mm(rest_hot(row0, q, 16), rest0)
        b = mm(hot1, em[:, cols]) + mm(rest_hot(row1, q, 16), rest1)
        out[:, cols] = (share0 * a + share1 * b).astype(BF16)

    give_main.wait_send()
    give_rest.wait_send()

    tail_y().wait_send()
    tail_give_y().wait_send()

    def finish(b, _):
        go_y(b).wait_send()
        give_y(b).wait_send()

        @pl.when((b <= z) & jnp.logical_not(last))
        def _():
            go_right(b).wait_send()
            tail_right(b).wait_send()

        @pl.when((b >= z) & jnp.logical_not(first))
        def _():
            go_left(b).wait_send()
            tail_left(b).wait_send()

        @pl.when(b > z)
        def _():
            give_right(b).wait_send()
            tail_give_right(b).wait_send()

        @pl.when(b < z)
        def _():
            give_left(b).wait_send()
            tail_give_left(b).wait_send()

        return 0

    lax.fori_loop(0, nz, finish, 0)


def shards(n, tokens, expert_ids, route_weight, w_gate, w_up, w_down, round_bits):
    nz = n // 2
    D = tokens.shape[1]
    F = w_gate.shape[2]
    wide = D + D // PACK
    cut = wide - wide // 128 // 6 * 128
    vmem = pl.BlockSpec(memory_space=pltpu.VMEM)
    hbm = pl.BlockSpec(memory_space=pl.ANY)
    dma = pltpu.SemaphoreType.DMA
    return pl.pallas_call(
        functools.partial(kernel, n, cut),
        out_shape=jax.ShapeDtypeStruct((tokens.shape[0], D // 2), BF16),
        in_specs=[vmem] * 4 + [hbm] * 3,
        out_specs=vmem,
        scratch_shapes=[
            pltpu.VMEM((D, F), BF16),
            pltpu.VMEM((D, F), BF16),
            pltpu.VMEM((F, D), BF16),
            pltpu.VMEM((n, MAIN, wide), BF16),
            pltpu.VMEM((PAIR, D), BF16),
            pltpu.VMEM((nz, PAIR, F), BF16),
            pltpu.VMEM((n, MAIN, wide), BF16),
            pltpu.VMEM((nz, MAIN, cut), BF16),
            pltpu.VMEM((nz + 1, MAIN, wide), BF16),
            pltpu.VMEM((nz + 1, MAIN, wide - cut), BF16),
            pltpu.VMEM((MAIN, wide - cut), BF16),
            pltpu.VMEM((MAIN, D // 2), BF16),
            pltpu.VMEM((16, D // PACK), BF16),
            dma((3,)),
        ] + [dma((nz,))] * 16 + [dma((2,))] * 4,
        compiler_params=pltpu.CompilerParams(
            collective_id=0, has_side_effects=True, vmem_limit_bytes=62 * 2**20
        ),
        cost_estimate=pl.CostEstimate(
            flops=6 * n * SLOT * D * F, bytes_accessed=6 * D * F, transcendentals=n * SLOT * F
        ),
    )(tokens, expert_ids.T, route_weight.T, round_bits, w_gate, w_up, w_down)


def solution(mesh):
    return jax.shard_map(
        functools.partial(shards, mesh.shape["tp"]),
        mesh=mesh,
        in_specs=(
            P(("parts", "tp"), None),
            P(("parts", "tp"), None),
            P(("parts", "tp"), None),
            P("ep", None, "tp"),
            P("ep", None, "tp"),
            P("ep", "tp", None),
            P("ep", "tp", None),
        ),
        out_specs=P(("parts", "tp"), "ep"),
        check_vma=False,
    )
```

```python
import functools

import jax
import jax.numpy as jnp
from jax import lax
from jax.experimental import pallas as pl
from jax.experimental.pallas import tpu as pltpu
from jax.sharding import PartitionSpec as P

SLOT = 36
MAIN = 32
REST = SLOT - MAIN
PACK = MAIN // REST
CHUNKS = 3
PAIR = 2 * MAIN + 16
F32 = jnp.float32
BF16 = jnp.bfloat16


def mm(a, b, dims=((1,), (0,))):
    return lax.dot_general(a, b, (dims, ((), ())), preferred_element_type=F32)


def one_hot(rows, cols, test):
    r = lax.broadcasted_iota(jnp.int32, (rows, cols), 0)
    c = lax.broadcasted_iota(jnp.int32, (rows, cols), 1)
    return jnp.where(test(r, c), 1.0, 0.0).astype(BF16)


def kernel(
    n, cut, tok, ids, wts, bits, wg_hbm, wu_hbm, wd_hbm, out,
    wg, wu, wd, X, xl, h, pb, yr, zr, zt, yt, em, ex,
    wsem, sR, sL, sY, rz, ry, sYr, rYr, sZ, rL, rR, sRt, sLt, rzt, sZt, rLt, rRt, st, rt, se, re,
):
    nz = n // 2
    t = lax.axis_index("tp")
    e = lax.axis_index("ep")
    z, y = t // 2, t % 2
    D = tok.shape[1]
    CH = D // PACK
    F = wg.shape[1]
    TOK = tok.shape[0]
    partner = t + 1 - 2 * y
    first, last = z == 0, z == nz - 1

    loads = [
        pltpu.make_async_copy(a.at[0], b, wsem.at[i])
        for i, (a, b) in enumerate(((wg_hbm, wg), (wu_hbm, wu), (wd_hbm, wd)))
    ]
    for c in loads:
        c.start()

    barrier = pltpu.get_barrier_semaphore()
    pl.semaphore_signal(barrier, inc=1, device_id={"tp": partner})
    pl.semaphore_signal(barrier, inc=1, device_id={"ep": 1 - e})

    @pl.when(jnp.logical_not(first))
    def _():
        pl.semaphore_signal(barrier, inc=1, device_id={"tp": t - 2})

    @pl.when(jnp.logical_not(last))
    def _():
        pl.semaphore_signal(barrier, inc=1, device_id={"tp": t + 2})

    tri = one_hot(TOK, TOK, lambda r, c: c <= r)

    def routing(expert):
        hit = ids[...] == expert
        share = jnp.sum(jnp.where(hit, wts[...], 0.0), axis=0, keepdims=True)
        named = jnp.sum(jnp.where(hit, 1.0, 0.0), axis=0, keepdims=True)
        share = jnp.broadcast_to(share, (TOK, TOK)).T[:, :1]
        named = jnp.broadcast_to(named, (TOK, TOK)).T
        count = mm(tri, named.astype(BF16))
        row = jnp.where(named > 0.5, count, 0.0).astype(jnp.int32) - 1
        return share, row

    def main_hot(row):
        c = lax.broadcasted_iota(jnp.int32, (TOK, MAIN), 1)
        return jnp.where(row[:, :MAIN] == c, 1.0, 0.0).astype(BF16)

    def rest_hot(row, q, width):
        c = lax.broadcasted_iota(jnp.int32, (TOK, width), 1)
        here = (c >= REST * q) & (c < REST * q + REST)
        return jnp.where(here & (row[:, :width] - MAIN == c - REST * q), 1.0, 0.0).astype(BF16)

    _, row = routing(e)
    hot = main_hot(row)
    rest = jnp.zeros((MAIN, CH), F32)
    for q in range(PACK):
        part = tok[:, q * CH:(q + 1) * CH]
        X[t, :, q * CH:(q + 1) * CH] = mm(hot, part, ((0,), (0,))).astype(BF16)
        rest = rest + mm(rest_hot(row, q, MAIN), part, ((0,), (0,)))
    X[t, :, D:] = rest.astype(BF16)

    neighbours = 4 - first.astype(jnp.int32) - last.astype(jnp.int32)
    pl.semaphore_wait(barrier, neighbours)

    step = cut // CHUNKS

    def span(k):
        return slice(k * step, (k + 1) * step) if k < CHUNKS else slice(cut, X.shape[2])

    def go_right(b, k):
        ref = X.at[2 * b + y, :, span(k)]
        return pltpu.make_async_remote_copy(ref, ref, sR.at[b, k], rz.at[b, k], device_id={"tp": t + 2})

    def go_left(b, k):
        ref = X.at[2 * b + y, :, span(k)]
        return pltpu.make_async_remote_copy(ref, ref, sL.at[b, k], rz.at[b, k], device_id={"tp": t - 2})

    def go_y(b, k):
        ref = X.at[2 * b + y, :, span(k)]
        return pltpu.make_async_remote_copy(ref, ref, sY.at[b, k], ry.at[b, k], device_id={"tp": partner})

    def tail_y():
        return pltpu.make_async_remote_copy(
            X.at[t, :, cut:], X.at[t, :, cut:], st.at[0], rt.at[0], device_id={"tp": partner})

    def tail_right(b):
        i = 2 * b + 1 - y
        return pltpu.make_async_remote_copy(
            X.at[i, :, cut:], X.at[i, :, cut:], sRt.at[b], rzt.at[b], device_id={"tp": t + 2})

    def tail_left(b):
        i = 2 * b + 1 - y
        return pltpu.make_async_remote_copy(
            X.at[i, :, cut:], X.at[i, :, cut:], sLt.at[b], rzt.at[b], device_id={"tp": t - 2})

    tail_y().start()
    for k in range(CHUNKS + 1):
        @pl.when(jnp.logical_not(last))
        def _():
            go_right(z, k).start()

        @pl.when(jnp.logical_not(first))
        def _():
            go_left(z, k).start()

        if k < CHUNKS:
            go_y(z, k).start()

    tail_y().wait_recv()

    @pl.when(jnp.logical_not(last))
    def _():
        tail_right(z).start()

    @pl.when(jnp.logical_not(first))
    def _():
        tail_left(z).start()

    def arrivals(d):
        a, b = z - d, z + d
        for k in range(CHUNKS + 1):
            @pl.when(a >= 0)
            def _():
                go_right(a, k).wait_recv()

                @pl.when(jnp.logical_not(last))
                def _():
                    go_right(a, k).start()

                if k < CHUNKS:
                    go_y(a, k).start()

            @pl.when(b < nz)
            def _():
                go_left(b, k).wait_recv()

                @pl.when(jnp.logical_not(first))
                def _():
                    go_left(b, k).start()

                if k < CHUNKS:
                    go_y(b, k).start()

        @pl.when(a >= 0)
        def _():
            tail_right(a).wait_recv()

            @pl.when(jnp.logical_not(last))
            def _():
                tail_right(a).start()

        @pl.when(b < nz)
        def _():
            tail_left(b).wait_recv()

            @pl.when(jnp.logical_not(first))
            def _():
                tail_left(b).start()

    def place(j):
        d = (j + 1) // 2
        return jnp.where(j % 2 == 1, z - d, z + d)

    def hidden(b):
        for k in range(CHUNKS):
            go_y(b, k).wait_recv()
        packed = X[pl.ds(2 * b, 2), :, D:].reshape(2 * MAIN, CH)
        for q in range(PACK):
            pick = one_hot(16, 2 * MAIN, lambda r, c: (r < 2 * REST) & (c == (r // REST) * MAIN + REST * q + r % REST))
            cols = slice(q * CH, (q + 1) * CH)
            xl[:2 * MAIN, cols] = X[pl.ds(2 * b, 2), :, cols].reshape(2 * MAIN, CH)
            xl[2 * MAIN:, cols] = mm(pick, packed).astype(BF16)

        def tile(i, _):
            cols = pl.ds(pl.multiple_of(i * 256, 256), 256)
            g = mm(xl[...], wg[:, cols])
            u = mm(xl[...], wu[:, cols])
            h[b, :, cols] = ((g / (1.0 + jnp.exp(-g))) * u).astype(BF16)
            return 0

        lax.fori_loop(0, F // 256, tile, 0)

    arrivals(1)
    loads[0].wait()
    loads[1].wait()

    def gather_step(j, _):
        d = (j + 1) // 2 + 1

        @pl.when((j % 2 == 1) & (d < nz))
        def _():
            arrivals(d)

        b = place(j)

        @pl.when((b >= 0) & (b < nz))
        def _():
            hidden(b)

        return 0

    lax.fori_loop(0, 2 * nz - 1, gather_step, 0)
    loads[2].wait()

    def give_y(b, k):
        return pltpu.make_async_remote_copy(
            pb.at[2 * b + 1 - y, :, span(k)], yr.at[b, :, span(k)], sYr.at[b, k], rYr.at[b, k],
            device_id={"tp": partner})

    def give_right(b, k):
        return pltpu.make_async_remote_copy(
            pb.at[2 * b + y, :, span(k)], zr.at[b + 1, :, span(k)], sZ.at[b, k], rL.at[b, k],
            device_id={"tp": t + 2})

    def give_left(b, k):
        return pltpu.make_async_remote_copy(
            pb.at[2 * b + y, :, span(k)], zr.at[b, :, span(k)], sZ.at[b, k], rR.at[b, k],
            device_id={"tp": t - 2})

    def tail_give_right(b):
        return pltpu.make_async_remote_copy(
            pb.at[2 * b + 1 - y, :, cut:], zt.at[b + 1], sZt.at[b], rLt.at[b], device_id={"tp": t + 2})

    def tail_give_left(b):
        return pltpu.make_async_remote_copy(
            pb.at[2 * b + 1 - y, :, cut:], zt.at[b], sZt.at[b], rRt.at[b], device_id={"tp": t - 2})

    def tail_give_y():
        return pltpu.make_async_remote_copy(
            pb.at[partner, :, cut:], yt, st.at[1], rt.at[1], device_id={"tp": partner})

    low16 = (bits[0] & 65535).astype(F32)

    def row_noise(b):
        shape = (PAIR, n * SLOT)
        r = lax.broadcasted_iota(jnp.int32, shape, 0)
        c = lax.broadcasted_iota(jnp.int32, shape, 1) - 2 * SLOT * b
        k = r - 2 * MAIN
        main = (r // MAIN) * SLOT + r % MAIN
        rest = (k // REST) * SLOT + MAIN + k % REST
        source = jnp.where(r < 2 * MAIN, main, jnp.where(k < 2 * REST, rest, -n * SLOT - 1))
        picked = jnp.where(source == c, jnp.broadcast_to(low16, shape), 0.0)
        return jnp.sum(picked, axis=1, keepdims=True).astype(jnp.int32)

    def down(b):
        noise = row_noise(b)
        rest = jnp.zeros((2 * MAIN, CH), F32)
        for q in range(PACK):
            cols = slice(q * CH, (q + 1) * CH)
            part = mm(h[b], wd[:, cols])
            c = lax.broadcasted_iota(jnp.int32, (PAIR, CH), 1) + q * CH
            low = (noise + 40503 * c) & 65535
            part = (part * (0.5 + low.astype(F32) / 65536.0)).astype(BF16)
            pb[pl.ds(2 * b, 2), :, cols] = part[:2 * MAIN].reshape(2, MAIN, CH)
            put = one_hot(2 * MAIN, 16, lambda r, c: (c < 2 * REST) & (r == (c // REST) * MAIN + REST * q + c % REST))
            rest = rest + mm(put, part[2 * MAIN:])
            for k in range(CHUNKS):
                if q * CH < (k + 1) * step <= (q + 1) * CH:
                    give_y(b, k).start()
        pb[pl.ds(2 * b, 2), :, D:] = rest.astype(BF16).reshape(2, MAIN, CH)

    def add_in(i, start, stop, terms):
        for c in range(start, stop, 384):
            size = min(384, stop - c)
            total = pb[i, :, c:c + size].astype(F32)
            for ref, k, base in terms:
                total = total + ref[k, :, c - base:c - base + size].astype(F32)
            pb[i, :, c:c + size] = total.astype(BF16)

    wide = pb.shape[2]

    def reduce(b):
        mine, other = 2 * b + y, 2 * b + 1 - y
        from_left = (b >= z) & jnp.logical_not(first)
        from_right = (b <= z) & jnp.logical_not(last)
        only_left = from_left & jnp.logical_not(from_right)
        only_right = from_right & jnp.logical_not(from_left)
        both = from_left & from_right
        none = jnp.logical_not(from_left) & jnp.logical_not(from_right)

        @pl.when(from_left)
        def _():
            tail_give_right(b).wait_recv()

        @pl.when(from_right)
        def _():
            tail_give_left(b).wait_recv()

        @pl.when(only_left)
        def _():
            add_in(other, cut, wide, ((zt, b + 1, cut),))

        @pl.when(only_right)
        def _():
            add_in(other, cut, wide, ((zt, b, cut),))

        @pl.when(both)
        def _():
            add_in(other, cut, wide, ((zt, b + 1, cut), (zt, b, cut)))

        @pl.when(b > z)
        def _():
            tail_give_right(b).start()

        @pl.when(b < z)
        def _():
            tail_give_left(b).start()

        @pl.when(b == z)
        def _():
            tail_give_y().start()

        for k in (CHUNKS,) + tuple(range(CHUNKS)):
            at, end = span(k).start, span(k).stop
            own = ((yr, b, 0),) if k < CHUNKS else ()
            if k < CHUNKS:
                give_y(b, k).wait_recv()

            @pl.when(from_left)
            def _():
                give_right(b, k).wait_recv()

            @pl.when(from_right)
            def _():
                give_left(b, k).wait_recv()

            if k < CHUNKS:
                @pl.when(none)
                def _():
                    add_in(mine, at, end, own)

            @pl.when(only_left)
            def _():
                add_in(mine, at, end, own + ((zr, b + 1, 0),))

            @pl.when(only_right)
            def _():
                add_in(mine, at, end, own + ((zr, b, 0),))

            @pl.when(both)
            def _():
                add_in(mine, at, end, own + ((zr, b + 1, 0), (zr, b, 0)))

            @pl.when(b > z)
            def _():
                give_right(b, k).start()

            @pl.when(b < z)
            def _():
                give_left(b, k).start()

    steps, lag = 2 * nz - 1, 3

    def down_step(i, _):
        b = place(jnp.maximum(steps - 1 - i, 0))

        @pl.when((i < steps) & (b >= 0) & (b < nz))
        def _():
            down(b)

        k = place(jnp.minimum(steps - 1 - i + lag, steps - 1))

        @pl.when((i >= lag) & (k >= 0) & (k < nz))
        def _():
            reduce(k)

        return 0

    lax.fori_loop(0, steps + lag, down_step, 0)
    tail_give_y().wait_recv()
    for c in range(cut, wide, 384):
        size = min(384, wide - c)
        pb[t, :, c:c + size] = (
            pb[t, :, c:c + size].astype(F32) + yt[:, c - cut:c - cut + size].astype(F32)
        ).astype(BF16)

    half = D // 2
    theirs = pl.ds(pl.multiple_of((1 - e) * half, 128), half)
    give_main = pltpu.make_async_remote_copy(
        pb.at[t, :, theirs], em, se.at[0], re.at[0], device_id={"ep": 1 - e})
    give_rest = pltpu.make_async_remote_copy(
        pb.at[t, pl.ds(pl.multiple_of((1 - e) * 16, 16), 16), D:], ex, se.at[1], re.at[1], device_id={"ep": 1 - e})
    give_main.start()
    give_rest.start()
    share0, row0 = routing(e)
    share1, row1 = routing(1 - e)
    hot0, hot1 = main_hot(row0), main_hot(row1)
    give_main.wait_recv()
    give_rest.wait_recv()
    rest0 = pb[t, pl.ds(pl.multiple_of(e * 16, 16), 16), D:]
    rest1 = ex[...]
    for q in range(PACK // 2):
        cols = slice(q * CH, (q + 1) * CH)
        own = pl.ds(pl.multiple_of(e * half + q * CH, 128), CH)
        a = mm(hot0, pb[t, :, own]) + mm(rest_hot(row0, q, 16), rest0)
        b = mm(hot1, em[:, cols]) + mm(rest_hot(row1, q, 16), rest1)
        out[:, cols] = (share0 * a + share1 * b).astype(BF16)

    give_main.wait_send()
    give_rest.wait_send()

    tail_y().wait_send()
    tail_give_y().wait_send()

    def finish(b, _):
        for k in range(CHUNKS):
            go_y(b, k).wait_send()
            give_y(b, k).wait_send()

        @pl.when((b <= z) & jnp.logical_not(last))
        def _():
            for k in range(CHUNKS + 1):
                go_right(b, k).wait_send()
            tail_right(b).wait_send()

        @pl.when((b >= z) & jnp.logical_not(first))
        def _():
            for k in range(CHUNKS + 1):
                go_left(b, k).wait_send()
            tail_left(b).wait_send()

        @pl.when(b > z)
        def _():
            for k in range(CHUNKS + 1):
                give_right(b, k).wait_send()
            tail_give_right(b).wait_send()

        @pl.when(b < z)
        def _():
            for k in range(CHUNKS + 1):
                give_left(b, k).wait_send()
            tail_give_left(b).wait_send()

        return 0

    lax.fori_loop(0, nz, finish, 0)


def shards(n, tokens, expert_ids, route_weight, w_gate, w_up, w_down, round_bits):
    nz = n // 2
    D = tokens.shape[1]
    F = w_gate.shape[2]
    wide = D + D // PACK
    lanes = wide // 128
    cut = (lanes - lanes // 6) // CHUNKS * CHUNKS * 128
    vmem = pl.BlockSpec(memory_space=pltpu.VMEM)
    hbm = pl.BlockSpec(memory_space=pl.ANY)
    dma = pltpu.SemaphoreType.DMA
    return pl.pallas_call(
        functools.partial(kernel, n, cut),
        out_shape=jax.ShapeDtypeStruct((tokens.shape[0], D // 2), BF16),
        in_specs=[vmem] * 4 + [hbm] * 3,
        out_specs=vmem,
        scratch_shapes=[
            pltpu.VMEM((D, F), BF16),
            pltpu.VMEM((D, F), BF16),
            pltpu.VMEM((F, D), BF16),
            pltpu.VMEM((n, MAIN, wide), BF16),
            pltpu.VMEM((PAIR, D), BF16),
            pltpu.VMEM((nz, PAIR, F), BF16),
            pltpu.VMEM((n, MAIN, wide), BF16),
            pltpu.VMEM((nz, MAIN, cut), BF16),
            pltpu.VMEM((nz + 1, MAIN, wide), BF16),
            pltpu.VMEM((nz + 1, MAIN, wide - cut), BF16),
            pltpu.VMEM((MAIN, wide - cut), BF16),
            pltpu.VMEM((MAIN, D // 2), BF16),
            pltpu.VMEM((16, D // PACK), BF16),
            dma((3,)),
        ] + [dma((nz, CHUNKS + 1))] * 10 + [dma((nz,))] * 6 + [dma((2,))] * 4,
        compiler_params=pltpu.CompilerParams(
            collective_id=0, has_side_effects=True, vmem_limit_bytes=62 * 2**20
        ),
        cost_estimate=pl.CostEstimate(
            flops=6 * n * SLOT * D * F, bytes_accessed=6 * D * F, transcendentals=n * SLOT * F
        ),
    )(tokens, expert_ids.T, route_weight.T, round_bits, w_gate, w_up, w_down)


def solution(mesh):
    return jax.shard_map(
        functools.partial(shards, mesh.shape["tp"]),
        mesh=mesh,
        in_specs=(
            P(("parts", "tp"), None),
            P(("parts", "tp"), None),
            P(("parts", "tp"), None),
            P("ep", None, "tp"),
            P("ep", None, "tp"),
            P("ep", "tp", None),
            P("ep", "tp", None),
        ),
        out_specs=P(("parts", "tp"), "ep"),
        check_vma=False,
    )
```

```python
import functools

import jax
import jax.numpy as jnp
from jax import lax
from jax.experimental import pallas as pl
from jax.experimental.pallas import tpu as pltpu
from jax.sharding import PartitionSpec as P

SLOT = 36
MAIN = 32
REST = SLOT - MAIN
PACK = MAIN // REST
CHUNKS = 3
PAIR = 2 * MAIN + 16
F32 = jnp.float32
BF16 = jnp.bfloat16


def mm(a, b, dims=((1,), (0,))):
    return lax.dot_general(a, b, (dims, ((), ())), preferred_element_type=F32)


def one_hot(rows, cols, test):
    r = lax.broadcasted_iota(jnp.int32, (rows, cols), 0)
    c = lax.broadcasted_iota(jnp.int32, (rows, cols), 1)
    return jnp.where(test(r, c), 1.0, 0.0).astype(BF16)


def kernel(
    n, cut, tok, ids, wts, bits, wg_hbm, wu_hbm, wd_hbm, out,
    wg, wu, wd, X, xl, ga, ua, h, pb, yr, zr, zt, yt, em, ex,
    wsem, sR, sL, sY, rz, ry, sYr, rYr, sZ, rL, rR, sRt, sLt, rzt, sZt, rLt, rRt, st, rt, se, re,
):
    nz = n // 2
    t = lax.axis_index("tp")
    e = lax.axis_index("ep")
    z, y = t // 2, t % 2
    D = tok.shape[1]
    CH = D // PACK
    F = wg.shape[1]
    TOK = tok.shape[0]
    partner = t + 1 - 2 * y
    first, last = z == 0, z == nz - 1

    loads = [
        pltpu.make_async_copy(a.at[0], b, wsem.at[i])
        for i, (a, b) in enumerate(((wg_hbm, wg), (wu_hbm, wu), (wd_hbm, wd)))
    ]
    for c in loads:
        c.start()

    barrier = pltpu.get_barrier_semaphore()
    pl.semaphore_signal(barrier, inc=1, device_id={"tp": partner})
    pl.semaphore_signal(barrier, inc=1, device_id={"ep": 1 - e})

    @pl.when(jnp.logical_not(first))
    def _():
        pl.semaphore_signal(barrier, inc=1, device_id={"tp": t - 2})

    @pl.when(jnp.logical_not(last))
    def _():
        pl.semaphore_signal(barrier, inc=1, device_id={"tp": t + 2})

    tri = one_hot(TOK, TOK, lambda r, c: c <= r)

    def routing(expert):
        hit = ids[...] == expert
        share = jnp.sum(jnp.where(hit, wts[...], 0.0), axis=0, keepdims=True)
        named = jnp.sum(jnp.where(hit, 1.0, 0.0), axis=0, keepdims=True)
        share = jnp.broadcast_to(share, (TOK, TOK)).T[:, :1]
        named = jnp.broadcast_to(named, (TOK, TOK)).T
        count = mm(tri, named.astype(BF16))
        row = jnp.where(named > 0.5, count, 0.0).astype(jnp.int32) - 1
        return share, row

    def main_hot(row):
        c = lax.broadcasted_iota(jnp.int32, (TOK, MAIN), 1)
        return jnp.where(row[:, :MAIN] == c, 1.0, 0.0).astype(BF16)

    def rest_hot(row, q, width):
        c = lax.broadcasted_iota(jnp.int32, (TOK, width), 1)
        here = (c >= REST * q) & (c < REST * q + REST)
        return jnp.where(here & (row[:, :width] - MAIN == c - REST * q), 1.0, 0.0).astype(BF16)

    neighbours = 4 - first.astype(jnp.int32) - last.astype(jnp.int32)
    pl.semaphore_wait(barrier, neighbours)

    step = cut // CHUNKS

    def span(k):
        return slice(k * step, (k + 1) * step) if k < CHUNKS else slice(cut, X.shape[2])

    def go_right(b, k):
        ref = X.at[2 * b + y, :, span(k)]
        return pltpu.make_async_remote_copy(ref, ref, sR.at[b, k], rz.at[b, k], device_id={"tp": t + 2})

    def go_left(b, k):
        ref = X.at[2 * b + y, :, span(k)]
        return pltpu.make_async_remote_copy(ref, ref, sL.at[b, k], rz.at[b, k], device_id={"tp": t - 2})

    def go_y(b, k):
        ref = X.at[2 * b + y, :, span(k)]
        return pltpu.make_async_remote_copy(ref, ref, sY.at[b, k], ry.at[b, k], device_id={"tp": partner})

    def tail_y():
        return pltpu.make_async_remote_copy(
            X.at[t, :, cut:], X.at[t, :, cut:], st.at[0], rt.at[0], device_id={"tp": partner})

    def tail_right(b):
        i = 2 * b + 1 - y
        return pltpu.make_async_remote_copy(
            X.at[i, :, cut:], X.at[i, :, cut:], sRt.at[b], rzt.at[b], device_id={"tp": t + 2})

    def tail_left(b):
        i = 2 * b + 1 - y
        return pltpu.make_async_remote_copy(
            X.at[i, :, cut:], X.at[i, :, cut:], sLt.at[b], rzt.at[b], device_id={"tp": t - 2})

    def send_own(k):
        @pl.when(jnp.logical_not(last))
        def _():
            go_right(z, k).start()

        @pl.when(jnp.logical_not(first))
        def _():
            go_left(z, k).start()

        if k < CHUNKS:
            go_y(z, k).start()

    _, row = routing(e)
    hot = main_hot(row)
    rest = jnp.zeros((MAIN, CH), F32)
    for q in range(PACK):
        part = tok[:, q * CH:(q + 1) * CH]
        X[t, :, q * CH:(q + 1) * CH] = mm(hot, part, ((0,), (0,))).astype(BF16)
        rest = rest + mm(rest_hot(row, q, MAIN), part, ((0,), (0,)))
        for k in range(CHUNKS):
            if q * CH < (k + 1) * step <= (q + 1) * CH:
                send_own(k)
    X[t, :, D:] = rest.astype(BF16)
    tail_y().start()
    send_own(CHUNKS)
    tail_y().wait_recv()

    @pl.when(jnp.logical_not(last))
    def _():
        tail_right(z).start()

    @pl.when(jnp.logical_not(first))
    def _():
        tail_left(z).start()

    def arrivals(d):
        a, b = z - d, z + d
        for k in range(CHUNKS + 1):
            @pl.when(a >= 0)
            def _():
                go_right(a, k).wait_recv()

                @pl.when(jnp.logical_not(last))
                def _():
                    go_right(a, k).start()

                if k < CHUNKS:
                    go_y(a, k).start()

            @pl.when(b < nz)
            def _():
                go_left(b, k).wait_recv()

                @pl.when(jnp.logical_not(first))
                def _():
                    go_left(b, k).start()

                if k < CHUNKS:
                    go_y(b, k).start()

        @pl.when(a >= 0)
        def _():
            tail_right(a).wait_recv()

            @pl.when(jnp.logical_not(last))
            def _():
                tail_right(a).start()

        @pl.when(b < nz)
        def _():
            tail_left(b).wait_recv()

            @pl.when(jnp.logical_not(first))
            def _():
                tail_left(b).start()

    def place(j):
        d = (j + 1) // 2
        return jnp.where(j % 2 == 1, z - d, z + d)

    def hidden(b):
        packed = X[pl.ds(2 * b, 2), :, D:].reshape(2 * MAIN, CH)
        for q in range(PACK):
            pick = one_hot(16, 2 * MAIN, lambda r, c: (r < 2 * REST) & (c == (r // REST) * MAIN + REST * q + r % REST))
            xl[2 * MAIN:, q * CH:(q + 1) * CH] = mm(pick, packed).astype(BF16)

        for k in range(CHUNKS):
            deep = slice(k * step, (k + 1) * step if k < CHUNKS - 1 else D)
            go_y(b, k).wait_recv()
            xl[:2 * MAIN, deep] = X[pl.ds(2 * b, 2), :, deep].reshape(2 * MAIN, deep.stop - deep.start)

            def tile(i, _):
                cols = pl.ds(pl.multiple_of(i * 256, 256), 256)
                g = mm(xl[:, deep], wg[deep, cols])
                u = mm(xl[:, deep], wu[deep, cols])
                if k > 0:
                    g = g + ga[:, cols]
                    u = u + ua[:, cols]
                if k < CHUNKS - 1:
                    ga[:, cols] = g
                    ua[:, cols] = u
                else:
                    h[b, :, cols] = ((g / (1.0 + jnp.exp(-g))) * u).astype(BF16)
                return 0

            lax.fori_loop(0, F // 256, tile, 0)

    arrivals(1)
    loads[0].wait()
    loads[1].wait()

    def gather_step(j, _):
        d = (j + 1) // 2 + 1

        @pl.when((j % 2 == 1) & (d < nz))
        def _():
            arrivals(d)

        b = place(j)

        @pl.when((b >= 0) & (b < nz))
        def _():
            hidden(b)

        return 0

    lax.fori_loop(0, 2 * nz - 1, gather_step, 0)
    loads[2].wait()

    def give_y(b, k):
        return pltpu.make_async_remote_copy(
            pb.at[2 * b + 1 - y, :, span(k)], yr.at[b, :, span(k)], sYr.at[b, k], rYr.at[b, k],
            device_id={"tp": partner})

    def give_right(b, k):
        return pltpu.make_async_remote_copy(
            pb.at[2 * b + y, :, span(k)], zr.at[b + 1, :, span(k)], sZ.at[b, k], rL.at[b, k],
            device_id={"tp": t + 2})

    def give_left(b, k):
        return pltpu.make_async_remote_copy(
            pb.at[2 * b + y, :, span(k)], zr.at[b, :, span(k)], sZ.at[b, k], rR.at[b, k],
            device_id={"tp": t - 2})

    def tail_give_right(b):
        return pltpu.make_async_remote_copy(
            pb.at[2 * b + 1 - y, :, cut:], zt.at[b + 1], sZt.at[b], rLt.at[b], device_id={"tp": t + 2})

    def tail_give_left(b):
        return pltpu.make_async_remote_copy(
            pb.at[2 * b + 1 - y, :, cut:], zt.at[b], sZt.at[b], rRt.at[b], device_id={"tp": t - 2})

    def tail_give_y():
        return pltpu.make_async_remote_copy(
            pb.at[partner, :, cut:], yt, st.at[1], rt.at[1], device_id={"tp": partner})

    low16 = (bits[0] & 65535).astype(F32)

    def row_noise(b):
        shape = (PAIR, n * SLOT)
        r = lax.broadcasted_iota(jnp.int32, shape, 0)
        c = lax.broadcasted_iota(jnp.int32, shape, 1) - 2 * SLOT * b
        k = r - 2 * MAIN
        main = (r // MAIN) * SLOT + r % MAIN
        rest = (k // REST) * SLOT + MAIN + k % REST
        source = jnp.where(r < 2 * MAIN, main, jnp.where(k < 2 * REST, rest, -n * SLOT - 1))
        picked = jnp.where(source == c, jnp.broadcast_to(low16, shape), 0.0)
        return jnp.sum(picked, axis=1, keepdims=True).astype(jnp.int32)

    def down(b):
        noise = row_noise(b)
        rest = jnp.zeros((2 * MAIN, CH), F32)
        for q in range(PACK):
            cols = slice(q * CH, (q + 1) * CH)
            part = mm(h[b], wd[:, cols])
            c = lax.broadcasted_iota(jnp.int32, (PAIR, CH), 1) + q * CH
            low = (noise + 40503 * c) & 65535
            part = (part * (0.5 + low.astype(F32) / 65536.0)).astype(BF16)
            pb[pl.ds(2 * b, 2), :, cols] = part[:2 * MAIN].reshape(2, MAIN, CH)
            put = one_hot(2 * MAIN, 16, lambda r, c: (c < 2 * REST) & (r == (c // REST) * MAIN + REST * q + c % REST))
            rest = rest + mm(put, part[2 * MAIN:])
            for k in range(CHUNKS):
                if q * CH < (k + 1) * step <= (q + 1) * CH:
                    give_y(b, k).start()
        pb[pl.ds(2 * b, 2), :, D:] = rest.astype(BF16).reshape(2, MAIN, CH)

    def add_in(i, start, stop, terms):
        for c in range(start, stop, 384):
            size = min(384, stop - c)
            total = pb[i, :, c:c + size].astype(F32)
            for ref, k, base in terms:
                total = total + ref[k, :, c - base:c - base + size].astype(F32)
            pb[i, :, c:c + size] = total.astype(BF16)

    wide = pb.shape[2]

    def reduce(b):
        mine, other = 2 * b + y, 2 * b + 1 - y
        from_left = (b >= z) & jnp.logical_not(first)
        from_right = (b <= z) & jnp.logical_not(last)
        only_left = from_left & jnp.logical_not(from_right)
        only_right = from_right & jnp.logical_not(from_left)
        both = from_left & from_right
        none = jnp.logical_not(from_left) & jnp.logical_not(from_right)

        @pl.when(from_left)
        def _():
            tail_give_right(b).wait_recv()

        @pl.when(from_right)
        def _():
            tail_give_left(b).wait_recv()

        @pl.when(only_left)
        def _():
            add_in(other, cut, wide, ((zt, b + 1, cut),))

        @pl.when(only_right)
        def _():
            add_in(other, cut, wide, ((zt, b, cut),))

        @pl.when(both)
        def _():
            add_in(other, cut, wide, ((zt, b + 1, cut), (zt, b, cut)))

        @pl.when(b > z)
        def _():
            tail_give_right(b).start()

        @pl.when(b < z)
        def _():
            tail_give_left(b).start()

        @pl.when(b == z)
        def _():
            tail_give_y().start()

        for k in (CHUNKS,) + tuple(range(CHUNKS)):
            at, end = span(k).start, span(k).stop
            own = ((yr, b, 0),) if k < CHUNKS else ()
            if k < CHUNKS:
                give_y(b, k).wait_recv()

            @pl.when(from_left)
            def _():
                give_right(b, k).wait_recv()

            @pl.when(from_right)
            def _():
                give_left(b, k).wait_recv()

            if k < CHUNKS:
                @pl.when(none)
                def _():
                    add_in(mine, at, end, own)

            @pl.when(only_left)
            def _():
                add_in(mine, at, end, own + ((zr, b + 1, 0),))

            @pl.when(only_right)
            def _():
                add_in(mine, at, end, own + ((zr, b, 0),))

            @pl.when(both)
            def _():
                add_in(mine, at, end, own + ((zr, b + 1, 0), (zr, b, 0)))

            @pl.when(b > z)
            def _():
                give_right(b, k).start()

            @pl.when(b < z)
            def _():
                give_left(b, k).start()

    steps, lag = 2 * nz - 1, 3

    def down_step(i, _):
        b = place(jnp.maximum(steps - 1 - i, 0))

        @pl.when((i < steps) & (b >= 0) & (b < nz))
        def _():
            down(b)

        k = place(jnp.minimum(steps - 1 - i + lag, steps - 1))

        @pl.when((i >= lag) & (k >= 0) & (k < nz))
        def _():
            reduce(k)

        return 0

    lax.fori_loop(0, steps + lag, down_step, 0)
    tail_give_y().wait_recv()
    for c in range(cut, wide, 384):
        size = min(384, wide - c)
        pb[t, :, c:c + size] = (
            pb[t, :, c:c + size].astype(F32) + yt[:, c - cut:c - cut + size].astype(F32)
        ).astype(BF16)

    half = D // 2
    theirs = pl.ds(pl.multiple_of((1 - e) * half, 128), half)
    give_main = pltpu.make_async_remote_copy(
        pb.at[t, :, theirs], em, se.at[0], re.at[0], device_id={"ep": 1 - e})
    give_rest = pltpu.make_async_remote_copy(
        pb.at[t, pl.ds(pl.multiple_of((1 - e) * 16, 16), 16), D:], ex, se.at[1], re.at[1], device_id={"ep": 1 - e})
    give_main.start()
    give_rest.start()
    share0, row0 = routing(e)
    share1, row1 = routing(1 - e)
    hot0, hot1 = main_hot(row0), main_hot(row1)
    give_main.wait_recv()
    give_rest.wait_recv()
    rest0 = pb[t, pl.ds(pl.multiple_of(e * 16, 16), 16), D:]
    rest1 = ex[...]
    for q in range(PACK // 2):
        cols = slice(q * CH, (q + 1) * CH)
        own = pl.ds(pl.multiple_of(e * half + q * CH, 128), CH)
        a = mm(hot0, pb[t, :, own]) + mm(rest_hot(row0, q, 16), rest0)
        b = mm(hot1, em[:, cols]) + mm(rest_hot(row1, q, 16), rest1)
        out[:, cols] = (share0 * a + share1 * b).astype(BF16)

    give_main.wait_send()
    give_rest.wait_send()

    tail_y().wait_send()
    tail_give_y().wait_send()

    def finish(b, _):
        for k in range(CHUNKS):
            go_y(b, k).wait_send()
            give_y(b, k).wait_send()

        @pl.when((b <= z) & jnp.logical_not(last))
        def _():
            for k in range(CHUNKS + 1):
                go_right(b, k).wait_send()
            tail_right(b).wait_send()

        @pl.when((b >= z) & jnp.logical_not(first))
        def _():
            for k in range(CHUNKS + 1):
                go_left(b, k).wait_send()
            tail_left(b).wait_send()

        @pl.when(b > z)
        def _():
            for k in range(CHUNKS + 1):
                give_right(b, k).wait_send()
            tail_give_right(b).wait_send()

        @pl.when(b < z)
        def _():
            for k in range(CHUNKS + 1):
                give_left(b, k).wait_send()
            tail_give_left(b).wait_send()

        return 0

    lax.fori_loop(0, nz, finish, 0)


def shards(n, tokens, expert_ids, route_weight, w_gate, w_up, w_down, round_bits):
    nz = n // 2
    D = tokens.shape[1]
    F = w_gate.shape[2]
    wide = D + D // PACK
    lanes = wide // 128
    cut = (lanes - lanes // 6) // CHUNKS * CHUNKS * 128
    vmem = pl.BlockSpec(memory_space=pltpu.VMEM)
    hbm = pl.BlockSpec(memory_space=pl.ANY)
    dma = pltpu.SemaphoreType.DMA
    return pl.pallas_call(
        functools.partial(kernel, n, cut),
        out_shape=jax.ShapeDtypeStruct((tokens.shape[0], D // 2), BF16),
        in_specs=[vmem] * 4 + [hbm] * 3,
        out_specs=vmem,
        scratch_shapes=[
            pltpu.VMEM((D, F), BF16),
            pltpu.VMEM((D, F), BF16),
            pltpu.VMEM((F, D), BF16),
            pltpu.VMEM((n, MAIN, wide), BF16),
            pltpu.VMEM((PAIR, D), BF16),
            pltpu.VMEM((PAIR, F), F32),
            pltpu.VMEM((PAIR, F), F32),
            pltpu.VMEM((nz, PAIR, F), BF16),
            pltpu.VMEM((n, MAIN, wide), BF16),
            pltpu.VMEM((nz, MAIN, cut), BF16),
            pltpu.VMEM((nz + 1, MAIN, wide), BF16),
            pltpu.VMEM((nz + 1, MAIN, wide - cut), BF16),
            pltpu.VMEM((MAIN, wide - cut), BF16),
            pltpu.VMEM((MAIN, D // 2), BF16),
            pltpu.VMEM((16, D // PACK), BF16),
            dma((3,)),
        ] + [dma((nz, CHUNKS + 1))] * 10 + [dma((nz,))] * 6 + [dma((2,))] * 4,
        compiler_params=pltpu.CompilerParams(
            collective_id=0, has_side_effects=True, vmem_limit_bytes=62 * 2**20
        ),
        cost_estimate=pl.CostEstimate(
            flops=6 * n * SLOT * D * F, bytes_accessed=6 * D * F, transcendentals=n * SLOT * F
        ),
    )(tokens, expert_ids.T, route_weight.T, round_bits, w_gate, w_up, w_down)


def solution(mesh):
    return jax.shard_map(
        functools.partial(shards, mesh.shape["tp"]),
        mesh=mesh,
        in_specs=(
            P(("parts", "tp"), None),
            P(("parts", "tp"), None),
            P(("parts", "tp"), None),
            P("ep", None, "tp"),
            P("ep", None, "tp"),
            P("ep", "tp", None),
            P("ep", "tp", None),
        ),
        out_specs=P(("parts", "tp"), "ep"),
        check_vma=False,
    )
```

```python
import functools

import jax
import jax.numpy as jnp
from jax import lax
from jax.experimental import pallas as pl
from jax.experimental.pallas import tpu as pltpu
from jax.sharding import PartitionSpec as P

SLOT = 36
MAIN = 32
REST = SLOT - MAIN
PACK = MAIN // REST
CHUNKS = 5
PAIR = 2 * MAIN + 16
F32 = jnp.float32
BF16 = jnp.bfloat16


def mm(a, b, dims=((1,), (0,))):
    return lax.dot_general(a, b, (dims, ((), ())), preferred_element_type=F32)


def one_hot(rows, cols, test):
    r = lax.broadcasted_iota(jnp.int32, (rows, cols), 0)
    c = lax.broadcasted_iota(jnp.int32, (rows, cols), 1)
    return jnp.where(test(r, c), 1.0, 0.0).astype(BF16)


def kernel(
    n, cut, tok, ids, wts, bits, wg_hbm, wu_hbm, wd_hbm, out,
    wg, wu, wd, X, xl, h, pb, yr, zr, zt, yt, em, ex,
    wsem, sR, sL, sY, rz, ry, sYr, rYr, sZ, rL, rR, sRt, sLt, rzt, sZt, rLt, rRt, st, rt, se, re,
):
    nz = n // 2
    t = lax.axis_index("tp")
    e = lax.axis_index("ep")
    z, y = t // 2, t % 2
    D = tok.shape[1]
    CH = D // PACK
    F = wg.shape[1]
    TOK = tok.shape[0]
    partner = t + 1 - 2 * y
    first, last = z == 0, z == nz - 1

    loads = [
        pltpu.make_async_copy(a.at[0], b, wsem.at[i])
        for i, (a, b) in enumerate(((wg_hbm, wg), (wu_hbm, wu), (wd_hbm, wd)))
    ]
    for c in loads:
        c.start()

    barrier = pltpu.get_barrier_semaphore()
    pl.semaphore_signal(barrier, inc=1, device_id={"tp": partner})
    pl.semaphore_signal(barrier, inc=1, device_id={"ep": 1 - e})

    @pl.when(jnp.logical_not(first))
    def _():
        pl.semaphore_signal(barrier, inc=1, device_id={"tp": t - 2})

    @pl.when(jnp.logical_not(last))
    def _():
        pl.semaphore_signal(barrier, inc=1, device_id={"tp": t + 2})

    tri = one_hot(TOK, TOK, lambda r, c: c <= r)

    def routing(expert):
        hit = ids[...] == expert
        share = jnp.sum(jnp.where(hit, wts[...], 0.0), axis=0, keepdims=True)
        named = jnp.sum(jnp.where(hit, 1.0, 0.0), axis=0, keepdims=True)
        share = jnp.broadcast_to(share, (TOK, TOK)).T[:, :1]
        named = jnp.broadcast_to(named, (TOK, TOK)).T
        count = mm(tri, named.astype(BF16))
        row = jnp.where(named > 0.5, count, 0.0).astype(jnp.int32) - 1
        return share, row

    def main_hot(row):
        c = lax.broadcasted_iota(jnp.int32, (TOK, MAIN), 1)
        return jnp.where(row[:, :MAIN] == c, 1.0, 0.0).astype(BF16)

    def rest_hot(row, q, width):
        c = lax.broadcasted_iota(jnp.int32, (TOK, width), 1)
        here = (c >= REST * q) & (c < REST * q + REST)
        return jnp.where(here & (row[:, :width] - MAIN == c - REST * q), 1.0, 0.0).astype(BF16)

    _, row = routing(e)
    hot = main_hot(row)
    rest = jnp.zeros((MAIN, CH), F32)
    for q in range(PACK):
        part = tok[:, q * CH:(q + 1) * CH]
        X[t, :, q * CH:(q + 1) * CH] = mm(hot, part, ((0,), (0,))).astype(BF16)
        rest = rest + mm(rest_hot(row, q, MAIN), part, ((0,), (0,)))
    X[t, :, D:] = rest.astype(BF16)

    neighbours = 4 - first.astype(jnp.int32) - last.astype(jnp.int32)
    pl.semaphore_wait(barrier, neighbours)

    step = cut // CHUNKS

    def span(k):
        return slice(k * step, (k + 1) * step) if k < CHUNKS else slice(cut, X.shape[2])

    def go_right(b, k):
        ref = X.at[2 * b + y, :, span(k)]
        return pltpu.make_async_remote_copy(ref, ref, sR.at[b, k], rz.at[b, k], device_id={"tp": t + 2})

    def go_left(b, k):
        ref = X.at[2 * b + y, :, span(k)]
        return pltpu.make_async_remote_copy(ref, ref, sL.at[b, k], rz.at[b, k], device_id={"tp": t - 2})

    def go_y(b, k):
        ref = X.at[2 * b + y, :, span(k)]
        return pltpu.make_async_remote_copy(ref, ref, sY.at[b, k], ry.at[b, k], device_id={"tp": partner})

    def tail_y():
        return pltpu.make_async_remote_copy(
            X.at[t, :, cut:], X.at[t, :, cut:], st.at[0], rt.at[0], device_id={"tp": partner})

    def tail_right(b):
        i = 2 * b + 1 - y
        return pltpu.make_async_remote_copy(
            X.at[i, :, cut:], X.at[i, :, cut:], sRt.at[b], rzt.at[b], device_id={"tp": t + 2})

    def tail_left(b):
        i = 2 * b + 1 - y
        return pltpu.make_async_remote_copy(
            X.at[i, :, cut:], X.at[i, :, cut:], sLt.at[b], rzt.at[b], device_id={"tp": t - 2})

    tail_y().start()
    for k in range(CHUNKS + 1):
        @pl.when(jnp.logical_not(last))
        def _():
            go_right(z, k).start()

        @pl.when(jnp.logical_not(first))
        def _():
            go_left(z, k).start()

        if k < CHUNKS:
            go_y(z, k).start()

    tail_y().wait_recv()

    @pl.when(jnp.logical_not(last))
    def _():
        tail_right(z).start()

    @pl.when(jnp.logical_not(first))
    def _():
        tail_left(z).start()

    def arrivals(d):
        a, b = z - d, z + d
        for k in range(CHUNKS + 1):
            @pl.when(a >= 0)
            def _():
                go_right(a, k).wait_recv()

                @pl.when(jnp.logical_not(last))
                def _():
                    go_right(a, k).start()

                if k < CHUNKS:
                    go_y(a, k).start()

            @pl.when(b < nz)
            def _():
                go_left(b, k).wait_recv()

                @pl.when(jnp.logical_not(first))
                def _():
                    go_left(b, k).start()

                if k < CHUNKS:
                    go_y(b, k).start()

        @pl.when(a >= 0)
        def _():
            tail_right(a).wait_recv()

            @pl.when(jnp.logical_not(last))
            def _():
                tail_right(a).start()

        @pl.when(b < nz)
        def _():
            tail_left(b).wait_recv()

            @pl.when(jnp.logical_not(first))
            def _():
                tail_left(b).start()

    def place(j):
        d = (j + 1) // 2
        return jnp.where(j % 2 == 1, z - d, z + d)

    def hidden(b):
        for k in range(CHUNKS):
            go_y(b, k).wait_recv()
        packed = X[pl.ds(2 * b, 2), :, D:].reshape(2 * MAIN, CH)
        for q in range(PACK):
            pick = one_hot(16, 2 * MAIN, lambda r, c: (r < 2 * REST) & (c == (r // REST) * MAIN + REST * q + r % REST))
            cols = slice(q * CH, (q + 1) * CH)
            xl[:2 * MAIN, cols] = X[pl.ds(2 * b, 2), :, cols].reshape(2 * MAIN, CH)
            xl[2 * MAIN:, cols] = mm(pick, packed).astype(BF16)

        def tile(i, _):
            cols = pl.ds(pl.multiple_of(i * 256, 256), 256)
            g = mm(xl[...], wg[:, cols])
            u = mm(xl[...], wu[:, cols])
            h[b, :, cols] = ((g / (1.0 + jnp.exp(-g))) * u).astype(BF16)
            return 0

        lax.fori_loop(0, F // 256, tile, 0)

    arrivals(1)
    loads[0].wait()
    loads[1].wait()

    def gather_step(j, _):
        d = (j + 1) // 2 + 1

        @pl.when((j % 2 == 1) & (d < nz))
        def _():
            arrivals(d)

        b = place(j)

        @pl.when((b >= 0) & (b < nz))
        def _():
            hidden(b)

        return 0

    lax.fori_loop(0, 2 * nz - 1, gather_step, 0)
    loads[2].wait()

    def give_y(b, k):
        return pltpu.make_async_remote_copy(
            pb.at[2 * b + 1 - y, :, span(k)], yr.at[b, :, span(k)], sYr.at[b, k], rYr.at[b, k],
            device_id={"tp": partner})

    def give_right(b, k):
        return pltpu.make_async_remote_copy(
            pb.at[2 * b + y, :, span(k)], zr.at[b + 1, :, span(k)], sZ.at[b, k], rL.at[b, k],
            device_id={"tp": t + 2})

    def give_left(b, k):
        return pltpu.make_async_remote_copy(
            pb.at[2 * b + y, :, span(k)], zr.at[b, :, span(k)], sZ.at[b, k], rR.at[b, k],
            device_id={"tp": t - 2})

    def tail_give_right(b):
        return pltpu.make_async_remote_copy(
            pb.at[2 * b + 1 - y, :, cut:], zt.at[b + 1], sZt.at[b], rLt.at[b], device_id={"tp": t + 2})

    def tail_give_left(b):
        return pltpu.make_async_remote_copy(
            pb.at[2 * b + 1 - y, :, cut:], zt.at[b], sZt.at[b], rRt.at[b], device_id={"tp": t - 2})

    def tail_give_y():
        return pltpu.make_async_remote_copy(
            pb.at[partner, :, cut:], yt, st.at[1], rt.at[1], device_id={"tp": partner})

    low16 = (bits[0] & 65535).astype(F32)

    def row_noise(b):
        shape = (PAIR, n * SLOT)
        r = lax.broadcasted_iota(jnp.int32, shape, 0)
        c = lax.broadcasted_iota(jnp.int32, shape, 1) - 2 * SLOT * b
        k = r - 2 * MAIN
        main = (r // MAIN) * SLOT + r % MAIN
        rest = (k // REST) * SLOT + MAIN + k % REST
        source = jnp.where(r < 2 * MAIN, main, jnp.where(k < 2 * REST, rest, -n * SLOT - 1))
        picked = jnp.where(source == c, jnp.broadcast_to(low16, shape), 0.0)
        return jnp.sum(picked, axis=1, keepdims=True).astype(jnp.int32)

    def down(b):
        noise = row_noise(b)
        rest = jnp.zeros((2 * MAIN, CH), F32)
        for q in range(PACK):
            cols = slice(q * CH, (q + 1) * CH)
            part = mm(h[b], wd[:, cols])
            c = lax.broadcasted_iota(jnp.int32, (PAIR, CH), 1) + q * CH
            low = (noise + 40503 * c) & 65535
            part = (part * (0.5 + low.astype(F32) / 65536.0)).astype(BF16)
            pb[pl.ds(2 * b, 2), :, cols] = part[:2 * MAIN].reshape(2, MAIN, CH)
            put = one_hot(2 * MAIN, 16, lambda r, c: (c < 2 * REST) & (r == (c // REST) * MAIN + REST * q + c % REST))
            rest = rest + mm(put, part[2 * MAIN:])
            for k in range(CHUNKS):
                if q * CH < (k + 1) * step <= (q + 1) * CH:
                    give_y(b, k).start()
        pb[pl.ds(2 * b, 2), :, D:] = rest.astype(BF16).reshape(2, MAIN, CH)

    def add_in(i, start, stop, terms):
        for c in range(start, stop, 384):
            size = min(384, stop - c)
            total = pb[i, :, c:c + size].astype(F32)
            for ref, k, base in terms:
                total = total + ref[k, :, c - base:c - base + size].astype(F32)
            pb[i, :, c:c + size] = total.astype(BF16)

    wide = pb.shape[2]

    def reduce(b):
        mine, other = 2 * b + y, 2 * b + 1 - y
        from_left = (b >= z) & jnp.logical_not(first)
        from_right = (b <= z) & jnp.logical_not(last)
        only_left = from_left & jnp.logical_not(from_right)
        only_right = from_right & jnp.logical_not(from_left)
        both = from_left & from_right
        none = jnp.logical_not(from_left) & jnp.logical_not(from_right)

        @pl.when(from_left)
        def _():
            tail_give_right(b).wait_recv()

        @pl.when(from_right)
        def _():
            tail_give_left(b).wait_recv()

        @pl.when(only_left)
        def _():
            add_in(other, cut, wide, ((zt, b + 1, cut),))

        @pl.when(only_right)
        def _():
            add_in(other, cut, wide, ((zt, b, cut),))

        @pl.when(both)
        def _():
            add_in(other, cut, wide, ((zt, b + 1, cut), (zt, b, cut)))

        @pl.when(b > z)
        def _():
            tail_give_right(b).start()

        @pl.when(b < z)
        def _():
            tail_give_left(b).start()

        @pl.when(b == z)
        def _():
            tail_give_y().start()

        for k in (CHUNKS,) + tuple(range(CHUNKS)):
            at, end = span(k).start, span(k).stop
            own = ((yr, b, 0),) if k < CHUNKS else ()
            if k < CHUNKS:
                give_y(b, k).wait_recv()

            @pl.when(from_left)
            def _():
                give_right(b, k).wait_recv()

            @pl.when(from_right)
            def _():
                give_left(b, k).wait_recv()

            if k < CHUNKS:
                @pl.when(none)
                def _():
                    add_in(mine, at, end, own)

            @pl.when(only_left)
            def _():
                add_in(mine, at, end, own + ((zr, b + 1, 0),))

            @pl.when(only_right)
            def _():
                add_in(mine, at, end, own + ((zr, b, 0),))

            @pl.when(both)
            def _():
                add_in(mine, at, end, own + ((zr, b + 1, 0), (zr, b, 0)))

            @pl.when(b > z)
            def _():
                give_right(b, k).start()

            @pl.when(b < z)
            def _():
                give_left(b, k).start()

    steps, lag = 2 * nz - 1, 3

    def down_step(i, _):
        b = place(jnp.maximum(steps - 1 - i, 0))

        @pl.when((i < steps) & (b >= 0) & (b < nz))
        def _():
            down(b)

        k = place(jnp.minimum(steps - 1 - i + lag, steps - 1))

        @pl.when((i >= lag) & (k >= 0) & (k < nz))
        def _():
            reduce(k)

        return 0

    lax.fori_loop(0, steps + lag, down_step, 0)
    tail_give_y().wait_recv()
    for c in range(cut, wide, 384):
        size = min(384, wide - c)
        pb[t, :, c:c + size] = (
            pb[t, :, c:c + size].astype(F32) + yt[:, c - cut:c - cut + size].astype(F32)
        ).astype(BF16)

    half = D // 2
    theirs = pl.ds(pl.multiple_of((1 - e) * half, 128), half)
    give_main = pltpu.make_async_remote_copy(
        pb.at[t, :, theirs], em, se.at[0], re.at[0], device_id={"ep": 1 - e})
    give_rest = pltpu.make_async_remote_copy(
        pb.at[t, pl.ds(pl.multiple_of((1 - e) * 16, 16), 16), D:], ex, se.at[1], re.at[1], device_id={"ep": 1 - e})
    give_main.start()
    give_rest.start()
    share0, row0 = routing(e)
    share1, row1 = routing(1 - e)
    hot0, hot1 = main_hot(row0), main_hot(row1)
    give_main.wait_recv()
    give_rest.wait_recv()
    rest0 = pb[t, pl.ds(pl.multiple_of(e * 16, 16), 16), D:]
    rest1 = ex[...]
    for q in range(PACK // 2):
        cols = slice(q * CH, (q + 1) * CH)
        own = pl.ds(pl.multiple_of(e * half + q * CH, 128), CH)
        a = mm(hot0, pb[t, :, own]) + mm(rest_hot(row0, q, 16), rest0)
        b = mm(hot1, em[:, cols]) + mm(rest_hot(row1, q, 16), rest1)
        out[:, cols] = (share0 * a + share1 * b).astype(BF16)

    give_main.wait_send()
    give_rest.wait_send()

    tail_y().wait_send()
    tail_give_y().wait_send()

    def finish(b, _):
        for k in range(CHUNKS):
            go_y(b, k).wait_send()
            give_y(b, k).wait_send()

        @pl.when((b <= z) & jnp.logical_not(last))
        def _():
            for k in range(CHUNKS + 1):
                go_right(b, k).wait_send()
            tail_right(b).wait_send()

        @pl.when((b >= z) & jnp.logical_not(first))
        def _():
            for k in range(CHUNKS + 1):
                go_left(b, k).wait_send()
            tail_left(b).wait_send()

        @pl.when(b > z)
        def _():
            for k in range(CHUNKS + 1):
                give_right(b, k).wait_send()
            tail_give_right(b).wait_send()

        @pl.when(b < z)
        def _():
            for k in range(CHUNKS + 1):
                give_left(b, k).wait_send()
            tail_give_left(b).wait_send()

        return 0

    lax.fori_loop(0, nz, finish, 0)


def shards(n, tokens, expert_ids, route_weight, w_gate, w_up, w_down, round_bits):
    nz = n // 2
    D = tokens.shape[1]
    F = w_gate.shape[2]
    wide = D + D // PACK
    lanes = wide // 128
    cut = (lanes - lanes // 6) // CHUNKS * CHUNKS * 128
    vmem = pl.BlockSpec(memory_space=pltpu.VMEM)
    hbm = pl.BlockSpec(memory_space=pl.ANY)
    dma = pltpu.SemaphoreType.DMA
    return pl.pallas_call(
        functools.partial(kernel, n, cut),
        out_shape=jax.ShapeDtypeStruct((tokens.shape[0], D // 2), BF16),
        in_specs=[vmem] * 4 + [hbm] * 3,
        out_specs=vmem,
        scratch_shapes=[
            pltpu.VMEM((D, F), BF16),
            pltpu.VMEM((D, F), BF16),
            pltpu.VMEM((F, D), BF16),
            pltpu.VMEM((n, MAIN, wide), BF16),
            pltpu.VMEM((PAIR, D), BF16),
            pltpu.VMEM((nz, PAIR, F), BF16),
            pltpu.VMEM((n, MAIN, wide), BF16),
            pltpu.VMEM((nz, MAIN, cut), BF16),
            pltpu.VMEM((nz + 1, MAIN, wide), BF16),
            pltpu.VMEM((nz + 1, MAIN, wide - cut), BF16),
            pltpu.VMEM((MAIN, wide - cut), BF16),
            pltpu.VMEM((MAIN, D // 2), BF16),
            pltpu.VMEM((16, D // PACK), BF16),
            dma((3,)),
        ] + [dma((nz, CHUNKS + 1))] * 10 + [dma((nz,))] * 6 + [dma((2,))] * 4,
        compiler_params=pltpu.CompilerParams(
            collective_id=0, has_side_effects=True, vmem_limit_bytes=62 * 2**20
        ),
        cost_estimate=pl.CostEstimate(
            flops=6 * n * SLOT * D * F, bytes_accessed=6 * D * F, transcendentals=n * SLOT * F
        ),
    )(tokens, expert_ids.T, route_weight.T, round_bits, w_gate, w_up, w_down)


def solution(mesh):
    return jax.shard_map(
        functools.partial(shards, mesh.shape["tp"]),
        mesh=mesh,
        in_specs=(
            P(("parts", "tp"), None),
            P(("parts", "tp"), None),
            P(("parts", "tp"), None),
            P("ep", None, "tp"),
            P("ep", None, "tp"),
            P("ep", "tp", None),
            P("ep", "tp", None),
        ),
        out_specs=P(("parts", "tp"), "ep"),
        check_vma=False,
    )
```
